32 devices in a mesh: dp: 8 (over y, x, core), fsdp: 4 (over z).
Axes of the slice: x: 2, y: 2, z: 4, core: 2. Of those that a mesh axis runs over, the one named last changes fastest.
Arguments:
- query: bfloat16 [1024, 4096], P('dp', 'fsdp'), may hold values from -6 to 6
- key: bfloat16 [1024, 4096], P('dp', 'fsdp'), may hold values from -6 to 6
- value: bfloat16 [1024, 4096], P('dp', 'fsdp'), may hold values from -6 to 6
- upstream: bfloat16 [1024, 4096], P('dp', 'fsdp'), may hold values from -480 to 480
- reward: int32 [1024], P('dp'), may hold values from -4 to 4
- lengths: int32 [4], replicated, may hold values from 1 to 16, 32 in all
- se_filter: bfloat16 [3, 7, 4096], P(None, None, 'fsdp'), may hold values from -2 to 2
- mr_filter: bfloat16 [128, 256], P(None, 'fsdp'), may hold values from -0.5 to 0.5
Outputs:
- grad_se: float32 [3, 7, 4096], P(None, None, 'fsdp')
- grad_mr: float32 [128, 256], P(None, 'fsdp')
The draws below stay inside these ranges and needn't reach their ends.
Inputs may be any that keep to these rules, and one draw needn't show every extreme that they name: The sequence packs 4 whole documents in order; entry i is the length of document i in blocks of 32 tokens; the lengths sum to 32 and the longest is exactly 16. A token's reward weight is its level divided by 4.
All inputs are finite; a program needn't handle non-finite values.
Results may differ from the reference program's by a relative error of at most 0.0041.
Values may be sent and summed in bfloat16 or wider, within the bound.
No kernel may reach another device: no remote copies, remote signals or barrier semaphores. Data moves between devices by JAX's collectives and lax.ppermute only.
A program may use at most 64 MiB of HBM per device.

```python
import math
import jax
import jax.numpy as jnp
import numpy as np
from jax import lax

CH = 4096
FGROUP = 16
GROUPS = 256
SELEN = 7
MRLEN = 128
BLOCK = 32
TOK_DEV = 128
NDOC = 4
SEQ = 1024
SEQ_BLOCKS = 32
N_FSDP = 4


def draw_upstream(key, part):
    first, second, third = jax.random.split(key, 3)
    rising = jnp.exp(jnp.log(3.0) * jnp.arange(CH, dtype=jnp.float32) / CH)
    channel_scale = rising * jnp.exp(jax.random.uniform(third, (CH,), jnp.float32, 0.0, jnp.log(4.0)))
    base = jnp.clip(jax.random.normal(first, (SEQ, CH), jnp.float32), -4.0, 4.0)
    row_scale = jnp.exp(jax.random.uniform(second, (SEQ, 1), jnp.float32, 0.0, jnp.log(10.0)))
    return (base * row_scale * channel_scale[None, :]).astype(jnp.bfloat16)


def with_ends(values, stream_key, smallest, top_value):
    longest = values.shape.index(max(values.shape))
    spots = []
    for shift in (0, 1):
        where = [jax.random.randint(jax.random.fold_in(stream_key, axis), (), 0, length) for axis, length in enumerate(values.shape)]
        where[longest] = (where[longest] + shift) % values.shape[longest]
        spots.append(tuple(where))
    return values.at[spots[0]].set(smallest).at[spots[1]].set(top_value)


def block_levels(own_key, shape, cuts, least, largest):
    level = 1.0
    for dim, shards_of in cuts:
        steps = jax.random.uniform(jax.random.fold_in(jax.random.fold_in(own_key, 6), dim), (shards_of,), jnp.float32, least / len(cuts), largest / len(cuts))
        level = level * jnp.repeat(jnp.exp(steps), shape[dim] // shards_of).reshape((-1,) + (1,) * (len(shape) - 1 - dim))
    return level


def length_profile(amount, total, limit, lean):
    portions = [(1 << 20) // math.isqrt(rank ** lean) + 1 for rank in range(2, amount + 1)]
    surplus, given = total - limit - (amount - 1), [1] * (amount - 1)
    while surplus > 0:
        movable = [i for i in range(amount - 1) if given[i] < limit]
        mass, left = sum([portions[i] for i in movable]), surplus
        for i in movable:
            more = min(limit - given[i], max(1, left * portions[i] // mass), surplus)
            given[i] = given[i] + more
            surplus = surplus - more
    return np.array([limit] + given)


def uneven_parts(rng, number_of, total, most, lean):
    if number_of == 2:
        one = jax.random.randint(rng, (), max(1, total - most), min(most, total - 1) + 1)
        return jnp.stack([one, total - one])
    sizes = jnp.asarray(length_profile(number_of, total, most, lean), jnp.int32)
    couples = (number_of - 1) // 2
    giver, taker = sizes[1:1 + 2 * couples:2], sizes[2:2 + 2 * couples:2]
    slack = jnp.minimum(giver - 1, most - taker)
    moved = jax.random.randint(jax.random.fold_in(rng, 1), (couples,), 0, 1 << 20) % (slack + 1)
    sizes = sizes.at[1:1 + 2 * couples:2].set(giver - moved).at[2:2 + 2 * couples:2].set(taker + moved)
    return sizes[jax.random.permutation(jax.random.fold_in(rng, 2), number_of)]


def noise(key, extent, scale, most, cuts=(), kind=jnp.bfloat16):
    values = jax.random.normal(key, extent, jnp.float32) * scale
    if len(cuts) > 0:
        values = block_levels(key, extent, cuts, -0.22, 0.18) * values
    return jnp.clip(values, min=-most, max=most).astype(kind)


def setup_inputs(seed: int = 0) -> dict:
    streams_of = jax.random.split(jax.random.key(seed), 9)
    query = noise(streams_of[0], (SEQ, CH), 1.0, 6.0, ((0, 8), (1, 4)))
    key = noise(streams_of[1], (SEQ, CH), 1.0, 6.0, ((0, 8), (1, 4)))
    value = noise(streams_of[2], (SEQ, CH), 1.0, 6.0, ((0, 8), (1, 4)))
    upstream = draw_upstream(jax.random.fold_in(streams_of[8], 71), 0)
    reward = with_ends(jax.random.randint(streams_of[4], (SEQ,), -4, 5), jax.random.fold_in(streams_of[4], 1), -4, 4).astype(jnp.int32)
    lengths = uneven_parts(streams_of[5], NDOC, SEQ_BLOCKS, SEQ_BLOCKS // 2, 1).astype(jnp.int32)
    se_filter = noise(streams_of[6], (3, SELEN, CH), SELEN ** -0.5, 2.0, ((2, 4),))
    mr_filter = noise(streams_of[7], (MRLEN, GROUPS), MRLEN ** -0.5, 0.5, ((1, 4),))
    return {"query": query, "key": key, "value": value, "upstream": upstream, "reward": reward, "lengths": lengths, "se_filter": se_filter, "mr_filter": mr_filter}


def block_docs(length_row, block_pos):
    ends = jnp.cumsum(length_row).astype(jnp.int32)
    counts = lax.optimization_barrier(jnp.sum((block_pos[:, None] >= ends[None, :]).astype(jnp.int32), axis=1)).astype(jnp.int32)
    return jnp.where(block_pos >= 0, counts, -1).astype(jnp.int32)

def band_matrix(vector, row_count):
    group_here, vec_len = vector.shape
    win_len = vec_len - 1
    tiled = jnp.tile(vector, (1, row_count))[:, :row_count * win_len]
    return tiled.reshape(group_here, row_count, win_len)

def forward_vector(medium_taps, block_rows):
    group_here = medium_taps.shape[1]
    head = jnp.zeros((group_here, 1), medium_taps.dtype)
    tail = jnp.zeros((group_here, block_rows), medium_taps.dtype)
    return jnp.concatenate([head, jnp.flip(medium_taps.T, axis=1), tail], axis=1)

def backward_vector(medium_taps, block_rows):
    group_here = medium_taps.shape[1]
    tail = jnp.zeros((group_here, block_rows + 1), medium_taps.dtype)
    return jnp.concatenate([medium_taps.T, tail], axis=1)

def diagonal_sums(products, filter_len):
    group_here, block_rows, win_len = products.shape
    flat = products.reshape(group_here, block_rows * win_len)
    flat = jnp.pad(flat, ((0, 0), (0, block_rows)))
    skewed = flat.reshape(group_here, block_rows, win_len + 1)
    totals = lax.optimization_barrier(jnp.sum(skewed[:, :, 1:filter_len + 1], axis=1))
    return jnp.flip(totals, axis=1).T

def block_windows(extended, sub_count, span_blocks, block_rows):
    channels = extended.shape[1]
    pieces = extended.reshape(sub_count + span_blocks, block_rows, channels)
    return jnp.stack([pieces[shift_idx:shift_idx + sub_count] for shift_idx in range(span_blocks + 1)], axis=1)

def short_filter(extended, token_docs, taps, row_count):
    edge = taps.shape[0] - 1
    result = jnp.zeros((row_count, extended.shape[1]), jnp.float32)
    for shift_idx in range(taps.shape[0]):
        begin = edge - shift_idx
        same_doc = (token_docs[edge:] == token_docs[begin:begin + row_count]).astype(jnp.float32)
        result = result + taps[shift_idx].astype(jnp.float32)[None, :] * extended[begin:begin + row_count].astype(jnp.float32) * same_doc[:, None]
    return result

def short_grads(cotangent, extended, token_docs, tap_count, row_count):
    edge = tap_count - 1
    rows_out = []
    for shift_idx in range(tap_count):
        begin = edge - shift_idx
        same_doc = (token_docs[edge:] == token_docs[begin:begin + row_count]).astype(jnp.float32)
        rows_out.append(lax.optimization_barrier(jnp.sum(cotangent * extended[begin:begin + row_count].astype(jnp.float32) * same_doc[:, None], axis=0)))
    return jnp.stack(rows_out, axis=0)

def reference(query, key, value, upstream, reward, lengths, se_filter, mr_filter):
    seq_rows = query.shape[0]
    slab_count = N_FSDP
    slab_width = CH // slab_count
    group_slab = GROUPS // slab_count
    block_rows = BLOCK
    filter_len = MRLEN
    edge = SELEN - 1
    sub_count = seq_rows // block_rows
    span_blocks = filter_len // block_rows
    win_len = block_rows + filter_len
    block_pos = jnp.arange(-span_blocks, sub_count + span_blocks, dtype=jnp.int32)
    docs_all = block_docs(lengths, block_pos)
    own_docs = docs_all[span_blocks:span_blocks + sub_count]
    fwd_mask = jnp.stack([own_docs == docs_all[idx:idx + sub_count] for idx in range(span_blocks + 1)], axis=1).astype(jnp.float32)
    bwd_mask = jnp.stack([own_docs == docs_all[span_blocks + idx:span_blocks + idx + sub_count] for idx in range(span_blocks + 1)], axis=1).astype(jnp.float32)
    token_docs = jnp.repeat(docs_all[span_blocks - 1:span_blocks + sub_count], block_rows)[block_rows - edge:]
    up_sq = lax.optimization_barrier(jnp.sum(jnp.square(upstream.astype(jnp.float32)), axis=1))
    inv_norm = lax.rsqrt(up_sq / CH + 1e-06)
    weight_rows = reward.astype(jnp.float32) * 0.25 * inv_norm

    def slabs(array):
        return jnp.transpose(array.reshape(seq_rows, slab_count, slab_width), (1, 0, 2))
    short_slabs = jnp.transpose(se_filter.reshape(3, SELEN, slab_count, slab_width), (2, 0, 1, 3))
    medium_slabs = jnp.transpose(mr_filter.reshape(MRLEN, slab_count, group_slab), (1, 0, 2))

    def per_slab(items):
        q_rows, k_rows, v_rows, up_rows, short_taps, medium_taps = items
        channels = q_rows.shape[1]
        group_all = medium_taps.shape[1]
        pad_rows = jnp.zeros((edge, channels), jnp.bfloat16)
        q_ext = jnp.concatenate([pad_rows, q_rows], axis=0)
        k_ext = jnp.concatenate([pad_rows, k_rows], axis=0)
        v_ext = jnp.concatenate([pad_rows, v_rows], axis=0)
        q_short = short_filter(q_ext, token_docs, short_taps[0], seq_rows)
        k_short = short_filter(k_ext, token_docs, short_taps[1], seq_rows)
        v_short = short_filter(v_ext, token_docs, short_taps[2], seq_rows)
        products = (k_short * v_short).astype(jnp.bfloat16)
        cotangent = weight_rows[:, None] * up_rows.astype(jnp.float32)
        dm_rows = (cotangent * q_short).astype(jnp.bfloat16)
        z_ext = jnp.concatenate([jnp.zeros((filter_len, channels), jnp.bfloat16), products], axis=0)
        z_win = block_windows(z_ext, sub_count, span_blocks, block_rows).astype(jnp.float32) * fwd_mask[:, :, None, None]
        z_win = z_win.reshape(sub_count, win_len, group_all, FGROUP)
        fwd_band = band_matrix(forward_vector(medium_taps, block_rows), block_rows).astype(jnp.float32)
        medium = jnp.einsum('gpr,nrgc->npgc', fwd_band, z_win, precision=lax.Precision.HIGHEST).reshape(seq_rows, channels)
        dm_ext = jnp.concatenate([dm_rows, jnp.zeros((filter_len, channels), jnp.bfloat16)], axis=0)
        dm_win = block_windows(dm_ext, sub_count, span_blocks, block_rows).astype(jnp.float32) * bwd_mask[:, :, None, None]
        dm_win = dm_win.reshape(sub_count, win_len, group_all, FGROUP)
        bwd_band = band_matrix(backward_vector(medium_taps, block_rows), block_rows).astype(jnp.float32)
        dz_rows = jnp.einsum('gpr,nrgc->npgc', bwd_band, dm_win, precision=lax.Precision.HIGHEST).reshape(seq_rows, channels)
        dm_four = dm_rows.astype(jnp.float32).reshape(sub_count, block_rows, group_all, FGROUP)
        pair = jnp.einsum('npgc,nrgc->gpr', dm_four, z_win, precision=lax.Precision.HIGHEST)
        grad_medium = diagonal_sums(pair, filter_len)
        cot_query = cotangent * medium
        cot_key = dz_rows * v_short
        cot_value = dz_rows * k_short
        grad_short = jnp.stack([short_grads(cot_query, q_ext, token_docs, SELEN, seq_rows), short_grads(cot_key, k_ext, token_docs, SELEN, seq_rows), short_grads(cot_value, v_ext, token_docs, SELEN, seq_rows)], axis=0)
        return (grad_short, grad_medium)
    short_all, medium_all = lax.map(per_slab, (slabs(query), slabs(key), slabs(value), slabs(upstream), short_slabs, medium_slabs))
    grad_se = jnp.transpose(short_all, (1, 2, 0, 3)).reshape(3, SELEN, CH)
    grad_mr = jnp.transpose(medium_all, (1, 0, 2)).reshape(MRLEN, GROUPS)
    return (grad_se / TOK_DEV, grad_mr / TOK_DEV)
```

```python
import functools

import jax
import jax.numpy as jnp
from jax import lax
from jax.experimental import pallas as pl
from jax.experimental.pallas import tpu as pltpu
from jax.sharding import PartitionSpec as P

BLOCK = 32
LANES = 128
TAIL = 16
PRE = 8
SLOT = PRE + BLOCK
F32 = jnp.float32
BF16 = jnp.bfloat16


def spec(space=pltpu.VMEM):
    return pl.BlockSpec(memory_space=space)


def dot(a, b, contract, precision=None):
    return lax.dot_general(
        a, b, ((contract[0], contract[1]), ((), ())), precision=precision, preferred_element_type=F32
    )


def pack_kernel(q_ref, k_ref, v_ref, up_ref, near_ref, far_ref, sq_ref):
    rows, channels = q_ref.shape
    near_ref[0:rows] = k_ref[...]
    near_ref[rows : 2 * rows] = v_ref[...]
    near_ref[2 * rows : 2 * rows + TAIL] = q_ref[rows - TAIL : rows]
    far_ref[0:TAIL] = k_ref[rows - TAIL : rows]
    far_ref[TAIL : 2 * TAIL] = v_ref[rows - TAIL : rows]
    total = jnp.zeros((rows, LANES), F32)
    for tile in range(channels // LANES):
        part = up_ref[:, tile * LANES : (tile + 1) * LANES].astype(F32)
        total = total + part * part
    sq_ref[...] = jnp.sum(total.T, axis=0, keepdims=True)


def band_kernel(h_ref, band_ref, band_t_ref, row_ref):
    taps, groups = h_ref.shape
    tiles = band_ref.shape[0]
    per_tile = groups // tiles
    width = band_ref.shape[2]
    tap = lax.broadcasted_iota(jnp.int32, (taps, width), 0)
    lane = lax.broadcasted_iota(jnp.int32, (taps, width), 1)
    flip = jnp.where(tap + lane == taps, 1.0, 0.0).astype(F32)
    row_ref[...] = dot(h_ref[...].astype(F32).T.astype(BF16), flip.astype(BF16), ((1,), (0,)))

    def one(tile, carry):
        rows = row_ref[pl.ds(pl.multiple_of(tile * per_tile, per_tile), per_tile), :]
        parts = [
            pltpu.roll(
                jnp.broadcast_to(rows[g : g + 1], (BLOCK, width)), 0, 1, stride=1, stride_axis=0
            )
            for g in range(per_tile)
        ]
        band = jnp.concatenate(parts, axis=0)
        band_ref[tile] = band.astype(BF16)
        band_t_ref[tile] = band.T[0 : taps + BLOCK].astype(BF16)
        return carry

    lax.fori_loop(0, tiles, one, 0)


def doc_of(lengths_ref, block):
    count = jnp.int32(0)
    end = jnp.int32(0)
    for i in range(lengths_ref.shape[0]):
        end = end + lengths_ref[i]
        count = count + jnp.where(block >= end, 1, 0)
    return jnp.where(block >= 0, count, -1)


def main_kernel(
    all_channels,
    lengths_ref,
    q_ref,
    k_ref,
    v_ref,
    up_ref,
    near_ref,
    far_ref,
    sq_ref,
    reward_ref,
    se_ref,
    band_ref,
    band_t_ref,
    out_ref,
    xq_ref,
    xk_ref,
    xv_ref,
    ks_ref,
    vs_ref,
    z_ref,
    zw_ref,
    dm_ref,
    dz_ref,
    cot_ref,
    w_ref,
):
    rows, channels = q_ref.shape
    own = rows // BLOCK
    taps = band_t_ref.shape[1] - BLOCK
    span = taps // BLOCK
    window = span + own
    tiles = channels // LANES
    per_tile = band_ref.shape[1] // BLOCK
    width = LANES // per_tile
    tap_count = se_ref.shape[1]

    first = lax.axis_index("dp") * own
    docs = [doc_of(lengths_ref, first + b) for b in range(-span - 1, own)]
    joined = [(docs[b + 1] == docs[b]) & (docs[b] >= 0) for b in range(window)]
    joined = [jnp.where(flag, 1.0, 0.0).astype(F32) for flag in joined]
    docs = docs[1:]
    same = [
        [jnp.where(docs[n + s] == docs[n + span], 1.0, 0.0).astype(F32) for s in range(span + 1)]
        for n in range(own)
    ]

    weight = (
        reward_ref[...].astype(F32) * 0.25 * lax.rsqrt(sq_ref[...] / all_channels + 1e-06)
    )
    w_ref[...] = jnp.broadcast_to(weight, (LANES, rows)).T

    lane_group = lax.broadcasted_iota(jnp.int32, (BLOCK, LANES), 1) // width
    picks = [lane_group == g for g in range(per_tile)]
    masks = [jnp.where(pick, 1.0, 0.0).astype(BF16) for pick in picks]
    row_index = lax.broadcasted_iota(jnp.int32, (per_tile * 8, 2 * LANES), 0)
    z_ref[window * BLOCK :] = jnp.zeros((z_ref.shape[0] - window * BLOCK, LANES), BF16)

    def fill(x_ref, pieces, before, first_block):
        for b, piece in enumerate(pieces):
            at = SLOT * b
            x_ref[at : at + PRE] = before * joined[first_block + b]
            x_ref[at + PRE : at + SLOT] = piece
            before = piece[BLOCK - PRE :]

    def shifted(x_ref, b, j):
        at = SLOT * b + PRE - j
        return x_ref[at : at + BLOCK, :]

    def short(x_ref, b, taps_now):
        total = taps_now[0:1] * shifted(x_ref, b, 0)
        for j in range(1, tap_count):
            total = total + taps_now[j : j + 1] * shifted(x_ref, b, j)
        return total

    def fold(x):
        return jnp.sum(x.reshape(BLOCK // 8, 8, LANES), axis=0)

    def one(tile, carry):
        at = pl.ds(pl.multiple_of(tile * LANES, LANES), LANES)
        q_taps = se_ref[0, :, at].astype(F32)
        k_taps = se_ref[1, :, at].astype(F32)
        v_taps = se_ref[2, :, at].astype(F32)

        def blocks_of(ref, start, count):
            return [
                ref[start + BLOCK * b : start + BLOCK * (b + 1), at].astype(F32) for b in range(count)
            ]

        q_before = near_ref[2 * rows : 2 * rows + TAIL, at].astype(F32)[TAIL - PRE :]
        k_before = far_ref[0:TAIL, at].astype(F32)[TAIL - PRE :]
        v_before = far_ref[TAIL : 2 * TAIL, at].astype(F32)[TAIL - PRE :]
        fill(xq_ref, blocks_of(q_ref, 0, own), q_before, span)
        fill(
            xk_ref,
            blocks_of(near_ref, rows - span * BLOCK, span) + blocks_of(k_ref, 0, own),
            k_before,
            0,
        )
        fill(
            xv_ref,
            blocks_of(near_ref, 2 * rows - span * BLOCK, span) + blocks_of(v_ref, 0, own),
            v_before,
            0,
        )
        for b in range(window):
            at_b = slice(BLOCK * b, BLOCK * (b + 1))
            ks = short(xk_ref, b, k_taps)
            vs = short(xv_ref, b, v_taps)
            ks_ref[at_b] = ks
            vs_ref[at_b] = vs
            z_ref[at_b] = (ks * vs).astype(BF16)
        for n in range(own):
            at_n = slice(BLOCK * n, BLOCK * (n + 1))
            cot = w_ref[at_n] * up_ref[at_n, at].astype(F32)
            cot_ref[at_n] = cot
            dm = (cot * short(xq_ref, n, q_taps)).astype(BF16)
            lanes = slice(LANES * (n % 2), LANES * (n % 2 + 1))
            for g in range(per_tile):
                dm_ref[n // 2, BLOCK * g : BLOCK * (g + 1), lanes] = dm * masks[g]
            for s in range(2 * LANES // BLOCK):
                piece = z_ref[BLOCK * (n + s) : BLOCK * (n + s + 1)]
                if s < span:
                    piece = piece * same[n][s].astype(BF16)
                zw_ref[n // 2, BLOCK * s : BLOCK * (s + 1), lanes] = piece

        band = band_ref[tile]
        band_t = band_t_ref[tile]
        pair = jnp.zeros((per_tile * BLOCK, 2 * LANES), F32)
        gq = [jnp.zeros((8, LANES), F32) for _ in range(tap_count)]
        dz_ref[...] = jnp.zeros_like(dz_ref)
        for half in range(own // 2):
            dms = dm_ref[half]
            zws = zw_ref[half]
            wide = dot(band, zws, ((1,), (0,)))
            back = dot(band_t, dms, ((1,), (0,)))
            pair = pair + dot(dms, zws, ((1,), (1,)))
            for side in range(2):
                n = 2 * half + side
                lanes = slice(LANES * side, LANES * (side + 1))
                m = wide[0:BLOCK, lanes]
                for g in range(1, per_tile):
                    m = jnp.where(picks[g], wide[BLOCK * g : BLOCK * (g + 1), lanes], m)
                cot_q = cot_ref[BLOCK * n : BLOCK * (n + 1)] * m
                for j in range(tap_count):
                    gq[j] = gq[j] + fold(cot_q * shifted(xq_ref, n, j))
                for s in range(span + 1):
                    at_s = slice(BLOCK * (n + s), BLOCK * (n + s + 1))
                    dz_ref[at_s] += back[BLOCK * s : BLOCK * (s + 1), lanes] * same[n][s]
        gk = [jnp.zeros((8, LANES), F32) for _ in range(tap_count)]
        gv = [jnp.zeros((8, LANES), F32) for _ in range(tap_count)]
        for b in range(window):
            at_b = slice(BLOCK * b, BLOCK * (b + 1))
            dz = dz_ref[at_b]
            cot_k = dz * vs_ref[at_b]
            cot_v = dz * ks_ref[at_b]
            for j in range(tap_count):
                gk[j] = gk[j] + fold(cot_k * shifted(xk_ref, b, j))
                gv[j] = gv[j] + fold(cot_v * shifted(xv_ref, b, j))
        for i, sums in enumerate((gq, gk, gv)):
            for j in range(tap_count):
                out_ref[8 * i + j : 8 * i + j + 1, at] = jnp.sum(sums[j], axis=0, keepdims=True)
            out_ref[8 * i + tap_count : 8 * i + 8, at] = jnp.zeros((8 - tap_count, LANES), F32)
        lined = pair.reshape(per_tile, BLOCK // 8, 8, 2 * LANES)
        skew = jnp.zeros((per_tile * 8, 2 * LANES), F32)
        for r in range(BLOCK // 8):
            rows_r = lined[:, r].reshape(per_tile * 8, 2 * LANES)
            skew = skew + pltpu.roll(rows_r, 2 * LANES - 1 - 8 * r, 1)
        for bit in range(3):
            moved = pltpu.roll(skew, 2 * LANES - (1 << bit), 1)
            skew = jnp.where((row_index >> bit) & 1 == 1, moved, skew)
        out_ref[24 : 24 + per_tile, at] = jnp.sum(
            skew[:, 0:LANES].reshape(per_tile, 8, LANES), axis=1
        )
        return carry

    lax.fori_loop(0, tiles, one, 0)


def last_kernel(scale, a_ref, b_ref, se_ref, mr_ref):
    total = (a_ref[...].astype(F32) + b_ref[...].astype(F32)) * scale
    tap_count = se_ref.shape[1]
    channels = total.shape[1]
    for i in range(3):
        se_ref[i] = total[8 * i : 8 * i + tap_count]
    flat = jnp.concatenate(
        [total[24:, t * LANES : (t + 1) * LANES] for t in range(channels // LANES)], axis=0
    )
    tap = lax.broadcasted_iota(jnp.int32, (LANES, LANES), 0)
    lane = lax.broadcasted_iota(jnp.int32, (LANES, LANES), 1)
    flip = jnp.where(tap + lane == LANES - 1, 1.0, 0.0).astype(F32)
    mr_ref[...] = dot(flip, flat, ((1,), (1,)), lax.Precision.HIGHEST)


def swapped(value, axis, distance):
    count = lax.axis_size(axis)
    return lax.ppermute(value, axis, [(i, i ^ distance) for i in range(count)])


def summed_small(value, axis):
    count = lax.axis_size(axis)
    if count & (count - 1):
        return lax.psum(value, axis)
    distance = 1
    while distance < count:
        value = value + swapped(value, axis, distance)
        distance *= 2
    return value


def moved_up(value, axis, steps):
    count = lax.axis_size(axis)
    return lax.ppermute(value, axis, [(i, i + steps) for i in range(count - steps)])


def on_device(query, key, value, upstream, reward, lengths, se_filter, mr_filter):
    rows, channels = query.shape
    taps, groups = mr_filter.shape
    tap_count = se_filter.shape[1]
    tiles = channels // LANES
    per_tile = groups // tiles
    stack = per_tile * BLOCK
    own = rows // BLOCK
    window = own + taps // BLOCK
    dp = lax.axis_size("dp")

    near, far, sq = pl.pallas_call(
        pack_kernel,
        out_shape=(
            jax.ShapeDtypeStruct((2 * rows + TAIL, channels), BF16),
            jax.ShapeDtypeStruct((2 * TAIL, channels), BF16),
            jax.ShapeDtypeStruct((1, rows), F32),
        ),
        in_specs=[spec()] * 4,
        out_specs=(spec(),) * 3,
        name="pack",
    )(query, key, value, upstream)
    near = moved_up(near, "dp", 1)
    far = moved_up(far, "dp", 2)
    sq = summed_small(sq, "fsdp")

    band, band_t = pl.pallas_call(
        band_kernel,
        out_shape=(
            jax.ShapeDtypeStruct((tiles, stack, 2 * LANES), BF16),
            jax.ShapeDtypeStruct((tiles, taps + BLOCK, stack), BF16),
        ),
        in_specs=[spec()],
        out_specs=(spec(),) * 2,
        scratch_shapes=[pltpu.VMEM((groups, 2 * LANES), F32)],
        name="band",
    )(mr_filter)

    part = pl.pallas_call(
        functools.partial(main_kernel, float(channels * lax.axis_size("fsdp"))),
        out_shape=jax.ShapeDtypeStruct((24 + per_tile, channels), F32),
        in_specs=[spec(pltpu.SMEM)] + [spec()] * 11,
        out_specs=spec(),
        scratch_shapes=[
            pltpu.VMEM((own * SLOT, LANES), F32),
            pltpu.VMEM((window * SLOT, LANES), F32),
            pltpu.VMEM((window * SLOT, LANES), F32),
            pltpu.VMEM((window * BLOCK, LANES), F32),
            pltpu.VMEM((window * BLOCK, LANES), F32),
            pltpu.VMEM(((own - 1) * BLOCK + 2 * LANES, LANES), BF16),
            pltpu.VMEM((own // 2, 2 * LANES, 2 * LANES), BF16),
            pltpu.VMEM((own // 2, stack, 2 * LANES), BF16),
            pltpu.VMEM((window * BLOCK, LANES), F32),
            pltpu.VMEM((rows, LANES), F32),
            pltpu.VMEM((rows, LANES), F32),
        ],
        compiler_params=pltpu.CompilerParams(vmem_limit_bytes=32 * 1024 * 1024),
        name="main",
    )(
        lengths,
        query,
        key,
        value,
        upstream,
        near,
        far,
        sq,
        reward.reshape(1, rows),
        se_filter,
        band,
        band_t,
    )

    if dp & (dp - 1):
        part = lax.psum(part, "dp")
        other = jnp.zeros_like(part)
    else:
        distance = 1
        other = jnp.zeros_like(part)
        while distance < dp:
            other = swapped(part, "dp", distance)
            distance *= 2
            if distance < dp:
                part = (part.astype(F32) + other.astype(F32)).astype(BF16)
    grad_se, grad_mr = pl.pallas_call(
        functools.partial(last_kernel, 1.0 / rows),
        out_shape=(
            jax.ShapeDtypeStruct((3, tap_count, channels), F32),
            jax.ShapeDtypeStruct((taps, groups), F32),
        ),
        in_specs=[spec()] * 2,
        out_specs=(spec(),) * 2,
        name="last",
    )(part, other)
    return grad_se, grad_mr


def solution(mesh):
    in_specs = (
        P("dp", "fsdp"),
        P("dp", "fsdp"),
        P("dp", "fsdp"),
        P("dp", "fsdp"),
        P("dp"),
        P(),
        P(None, None, "fsdp"),
        P(None, "fsdp"),
    )
    out_specs = (P(None, None, "fsdp"), P(None, "fsdp"))
    return jax.shard_map(
        on_device, mesh=mesh, in_specs=in_specs, out_specs=out_specs, check_vma=False
    )
```

```python
import functools

import jax
import jax.numpy as jnp
from jax import lax
from jax.experimental import pallas as pl
from jax.experimental.pallas import tpu as pltpu
from jax.sharding import PartitionSpec as P

BLOCK = 32
LANES = 128
TAIL = 16
PRE = 8
SLOT = PRE + BLOCK
LIMIT = 24 * 1024 * 1024
MOST = 60 * 1024 * 1024
F32 = jnp.float32
BF16 = jnp.bfloat16


def spec(space=pltpu.VMEM):
    return pl.BlockSpec(memory_space=space)


def dot(a, b, contract, precision=None):
    return lax.dot_general(
        a, b, ((contract[0], contract[1]), ((), ())), precision=precision, preferred_element_type=F32
    )


def doc_of(lengths_ref, block):
    count = jnp.int32(0)
    end = jnp.int32(0)
    for i in range(lengths_ref.shape[0]):
        end = end + lengths_ref[i]
        count = count + jnp.where(block >= end, 1, 0)
    return jnp.where(block >= 0, count, -1)


def first_kernel(
    span,
    lengths_ref,
    reward_ref,
    q_ref,
    k_ref,
    v_ref,
    up_ref,
    near_ref,
    far_ref,
    sq_ref,
    note_ref,
    up_here,
    near_here,
    sems,
):
    rows, channels = k_ref.shape
    tail = pl.ds(rows - TAIL, TAIL)
    k_rows, v_rows, q_rows = pl.ds(0, rows), pl.ds(rows, rows), pl.ds(2 * rows, TAIL)
    coming = [
        pltpu.make_async_copy(source, target, sems.at[i])
        for i, (source, target) in enumerate(
            (
                (k_ref, near_here.at[k_rows]),
                (v_ref, near_here.at[v_rows]),
                (q_ref.at[tail], near_here.at[q_rows]),
                (up_ref, up_here),
            )
        )
    ]
    going = [
        pltpu.make_async_copy(source, target, sems.at[4 + i])
        for i, (source, target) in enumerate(
            (
                (near_here, near_ref),
                (near_here.at[pl.ds(rows - TAIL, TAIL)], far_ref.at[pl.ds(0, TAIL)]),
                (near_here.at[pl.ds(2 * rows - TAIL, TAIL)], far_ref.at[pl.ds(TAIL, TAIL)]),
            )
        )
    ]
    for copy in coming:
        copy.start()
    own = rows // BLOCK
    window = span + own
    first = lax.axis_index("dp") * own
    docs = [doc_of(lengths_ref, first + b) for b in range(-span - 1, own)]
    notes = [(docs[b + 1] == docs[b]) & (docs[b] >= 0) for b in range(window)]
    docs = docs[1:]
    notes = notes + [docs[n + s] == docs[n + span] for n in range(own) for s in range(span)]
    for i, note in enumerate(notes):
        note_ref[i : i + 1] = jnp.full((1, rows), jnp.where(note, 1.0, 0.0).astype(F32))
    note_ref[len(notes) : len(notes) + 1] = reward_ref[...].astype(F32) * 0.25
    for copy in coming[0:3]:
        copy.wait()
    for copy in going:
        copy.start()
    coming[3].wait()
    total = jnp.zeros((rows, LANES), F32)
    for tile in range(channels // LANES):
        part = up_here[:, tile * LANES : (tile + 1) * LANES].astype(F32)
        total = total + part * part
    sq_ref[...] = jnp.sum(total.T, axis=0, keepdims=True)
    for copy in going:
        copy.wait()


def band_kernel(h_ref, band_ref, band_t_ref, row_ref):
    groups, taps = h_ref.shape
    tiles = band_ref.shape[0]
    per_tile = groups // tiles
    width = band_ref.shape[2]
    tap = lax.broadcasted_iota(jnp.int32, (taps, width), 0)
    lane = lax.broadcasted_iota(jnp.int32, (taps, width), 1)
    flip = jnp.where(tap + lane == taps, 1.0, 0.0).astype(F32)
    row_ref[...] = dot(h_ref[...], flip.astype(BF16), ((1,), (0,)))

    def one(tile, carry):
        rows = row_ref[pl.ds(pl.multiple_of(tile * per_tile, per_tile), per_tile), :]
        parts = [
            pltpu.roll(
                jnp.broadcast_to(rows[g : g + 1], (BLOCK, width)), 0, 1, stride=1, stride_axis=0
            )
            for g in range(per_tile)
        ]
        band = jnp.concatenate(parts, axis=0)
        band_ref[tile] = band.astype(BF16)
        band_t_ref[tile] = band.T[0 : taps + BLOCK].astype(BF16)
        return carry

    lax.fori_loop(0, tiles, one, 0)


def main_kernel(
    all_channels,
    q_ref,
    k_ref,
    v_ref,
    up_ref,
    near_ref,
    far_ref,
    sq_ref,
    note_ref,
    se_ref,
    band_ref,
    band_t_ref,
    out_ref,
    xq_ref,
    xk_ref,
    xv_ref,
    ks_ref,
    vs_ref,
    z_ref,
    zw_ref,
    dm_ref,
    dz_ref,
    cot_ref,
    skew_ref,
    w_ref,
):
    rows, channels = q_ref.shape
    own = rows // BLOCK
    taps = band_t_ref.shape[1] - BLOCK
    span = taps // BLOCK
    window = span + own
    tiles = channels // LANES
    per_tile = band_ref.shape[1] // BLOCK
    width = LANES // per_tile
    tap_count = se_ref.shape[1]

    joined = [note_ref[b : b + 1, 0:LANES] for b in range(window)]
    same = [
        [note_ref[window + n * span + s : window + n * span + s + 1, 0:LANES] for s in range(span)]
        for n in range(own)
    ]
    reward_row = window + own * span
    weight = note_ref[reward_row : reward_row + 1] * lax.rsqrt(sq_ref[...] / all_channels + 1e-06)
    w_ref[...] = jnp.broadcast_to(weight, (LANES, rows)).T

    lane_group = lax.broadcasted_iota(jnp.int32, (BLOCK, LANES), 1) // width
    picks = [lane_group == g for g in range(per_tile)]
    masks = [jnp.where(pick, 1.0, 0.0).astype(BF16) for pick in picks]
    beside = z_ref.shape[0]
    for side in range(beside):
        z_ref[side, window * BLOCK :] = jnp.zeros((z_ref.shape[1] - window * BLOCK, LANES), BF16)

    def fill(x_ref, side, pieces, before, first_block):
        for b, piece in enumerate(pieces):
            at = SLOT * b
            x_ref[side, at : at + PRE] = before * joined[first_block + b]
            x_ref[side, at + PRE : at + SLOT] = piece
            before = piece[BLOCK - PRE :]

    def shifted(x_ref, side, b, j):
        at = SLOT * b + PRE - j
        return x_ref[side, at : at + BLOCK, :]

    def short(x_ref, side, b, taps_now):
        total = taps_now[0:1] * shifted(x_ref, side, b, 0)
        for j in range(1, tap_count):
            total = total + taps_now[j : j + 1] * shifted(x_ref, side, b, j)
        return total

    def fold(x):
        return jnp.sum(x.reshape(BLOCK // 8, 8, LANES), axis=0)

    def first_half(tile, side):
        at = pl.ds(pl.multiple_of(tile * LANES, LANES), LANES)
        q_taps = se_ref[0, :, at].astype(F32)
        k_taps = se_ref[1, :, at].astype(F32)
        v_taps = se_ref[2, :, at].astype(F32)

        def blocks_of(ref, start, count):
            return [
                ref[start + BLOCK * b : start + BLOCK * (b + 1), at].astype(F32) for b in range(count)
            ]

        q_before = near_ref[2 * rows : 2 * rows + TAIL, at].astype(F32)[TAIL - PRE :]
        k_before = far_ref[0:TAIL, at].astype(F32)[TAIL - PRE :]
        v_before = far_ref[TAIL : 2 * TAIL, at].astype(F32)[TAIL - PRE :]
        k_halo = blocks_of(near_ref, rows - span * BLOCK, span)
        v_halo = blocks_of(near_ref, 2 * rows - span * BLOCK, span)
        fill(xk_ref, side, k_halo + blocks_of(k_ref, 0, own), k_before, 0)
        fill(xv_ref, side, v_halo + blocks_of(v_ref, 0, own), v_before, 0)
        fill(xq_ref, side, blocks_of(q_ref, 0, own), q_before, span)
        for b in range(window):
            at_b = slice(BLOCK * b, BLOCK * (b + 1))
            ks = short(xk_ref, side, b, k_taps)
            vs = short(xv_ref, side, b, v_taps)
            ks_ref[side, at_b] = ks
            vs_ref[side, at_b] = vs
            z_ref[side, at_b] = (ks * vs).astype(BF16)
        for n in range(own):
            at_n = slice(BLOCK * n, BLOCK * (n + 1))
            cot = w_ref[at_n] * up_ref[at_n, at].astype(F32)
            cot_ref[side, at_n] = cot
            dm = (cot * short(xq_ref, side, n, q_taps)).astype(BF16)
            lanes = slice(LANES * (n % 2), LANES * (n % 2 + 1))
            for g in range(per_tile):
                dm_ref[side, n // 2, BLOCK * g : BLOCK * (g + 1), lanes] = dm * masks[g]
            for s in range(2 * LANES // BLOCK):
                piece = z_ref[side, BLOCK * (n + s) : BLOCK * (n + s + 1)]
                if s < span:
                    piece = piece * same[n][s].astype(BF16)
                zw_ref[side, n // 2, BLOCK * s : BLOCK * (s + 1), lanes] = piece

    def middle(tile, side):
        band = band_ref[tile]
        band_t = band_t_ref[tile]
        pair = None
        gq = [jnp.zeros((8, LANES), F32) for _ in range(tap_count)]
        for half in range(own // 2):
            dms = dm_ref[side, half]
            zws = zw_ref[side, half]
            wide = dot(band, zws, ((1,), (0,)))
            back = dot(band_t, dms, ((1,), (0,)))
            both = dot(dms, zws, ((1,), (1,)))
            pair = both if pair is None else pair + both
            for part in range(2):
                n = 2 * half + part
                lanes = slice(LANES * part, LANES * (part + 1))
                m = wide[0:BLOCK, lanes]
                for g in range(1, per_tile):
                    m = jnp.where(picks[g], wide[BLOCK * g : BLOCK * (g + 1), lanes], m)
                cot_q = cot_ref[side, BLOCK * n : BLOCK * (n + 1)] * m
                for j in range(tap_count):
                    gq[j] = gq[j] + fold(cot_q * shifted(xq_ref, side, n, j))
                for s in range(span + 1):
                    at_s = slice(BLOCK * (n + s), BLOCK * (n + s + 1))
                    term = back[BLOCK * s : BLOCK * (s + 1), lanes]
                    if s < span:
                        term = term * same[n][s]
                    if n == 0 or s == span:
                        dz_ref[side, at_s] = term
                    else:
                        dz_ref[side, at_s] += term
        lined = pair.reshape(per_tile, BLOCK // 8, 8, 2 * LANES)
        skew = None
        for r in range(BLOCK // 8):
            rows_r = lined[:, r].reshape(per_tile * 8, 2 * LANES)
            moved = pltpu.roll(rows_r, 2 * LANES - 1 - 8 * r, 1)
            skew = moved if skew is None else skew + moved
        skew_ref[tile] = skew
        return gq

    def last_half(tile, side, gq):
        at = pl.ds(pl.multiple_of(tile * LANES, LANES), LANES)
        gk = [jnp.zeros((8, LANES), F32) for _ in range(tap_count)]
        gv = [jnp.zeros((8, LANES), F32) for _ in range(tap_count)]
        for b in range(window):
            at_b = slice(BLOCK * b, BLOCK * (b + 1))
            dz = dz_ref[side, at_b]
            cot_k = dz * vs_ref[side, at_b]
            cot_v = dz * ks_ref[side, at_b]
            for j in range(tap_count):
                gk[j] = gk[j] + fold(cot_k * shifted(xk_ref, side, b, j))
                gv[j] = gv[j] + fold(cot_v * shifted(xv_ref, side, b, j))
        for i, sums in enumerate((gq, gk, gv)):
            for j in range(tap_count):
                out_ref[8 * i + j : 8 * i + j + 1, at] = jnp.sum(sums[j], axis=0, keepdims=True)
            out_ref[8 * i + tap_count : 8 * i + 8, at] = jnp.zeros((8 - tap_count, LANES), F32)

    def some(step, carry):
        now = [step * beside + side for side in range(beside)]
        for side, tile in enumerate(now):
            first_half(tile, side)
        sums = [middle(tile, side) for side, tile in enumerate(now)]
        for side, tile in enumerate(now):
            last_half(tile, side, sums[side])
        return carry

    lax.fori_loop(0, tiles // beside, some, 0)
    skew = skew_ref[...].reshape(tiles * per_tile * 8, 2 * LANES)
    row_index = lax.broadcasted_iota(jnp.int32, skew.shape, 0)
    for bit in range(3):
        moved = pltpu.roll(skew, 2 * LANES - (1 << bit), 1)
        skew = jnp.where((row_index >> bit) & 1 == 1, moved, skew)
    totals = jnp.sum(skew[:, 0:LANES].reshape(tiles * per_tile, 8, LANES), axis=1)
    for tile in range(tiles):
        out_ref[24 : 24 + per_tile, LANES * tile : LANES * (tile + 1)] = totals[
            per_tile * tile : per_tile * (tile + 1)
        ]


def last_kernel(scale, *refs):
    *part_refs, se_ref, mr_ref = refs
    parts = [ref[...].astype(F32) for ref in part_refs]
    while len(parts) > 1:
        parts = [a + b for a, b in zip(parts[::2], parts[1::2])]
    total = parts[0] * scale
    tap_count = se_ref.shape[1]
    channels = total.shape[1]
    for i in range(3):
        se_ref[i] = total[8 * i : 8 * i + tap_count]
    flat = jnp.concatenate(
        [total[24:, t * LANES : (t + 1) * LANES] for t in range(channels // LANES)], axis=0
    )
    tap = lax.broadcasted_iota(jnp.int32, (LANES, LANES), 0)
    lane = lax.broadcasted_iota(jnp.int32, (LANES, LANES), 1)
    flip = jnp.where(tap + lane == LANES - 1, 1.0, 0.0).astype(F32)
    mr_ref[...] = dot(flat, flip, ((1,), (0,)), lax.Precision.HIGHEST)


def swapped(value, axis, distance):
    count = lax.axis_size(axis)
    return lax.ppermute(value, axis, [(i, i ^ distance) for i in range(count)])


def summed_small(value, axis):
    count = lax.axis_size(axis)
    if count & (count - 1):
        return lax.psum(value, axis)
    distance = 1
    while distance < count:
        value = value + swapped(value, axis, distance)
        distance *= 2
    return value


def spread(part, axis):
    count = lax.axis_size(axis)
    if count & (count - 1) or count < 8:
        return [lax.psum(part, axis)]
    mine = (part + swapped(part, axis, 1)).astype(BF16)
    distance = 8
    while distance < count:
        mine = (mine.astype(F32) + swapped(mine, axis, distance).astype(F32)).astype(BF16)
        distance *= 2
    return [mine] + [swapped(mine, axis, d) for d in (2, 4, 6)]


def moved_up(value, axis, steps):
    count = lax.axis_size(axis)
    return lax.ppermute(value, axis, [(i, (i + steps) % count) for i in range(count)])


def on_device(query, key, value, upstream, reward, lengths, se_filter, mr_filter):
    rows, channels = query.shape
    taps, groups = mr_filter.shape
    tap_count = se_filter.shape[1]
    tiles = channels // LANES
    per_tile = groups // tiles
    stack = per_tile * BLOCK
    own = rows // BLOCK
    window = own + taps // BLOCK
    beside = 2 if tiles % 2 == 0 else 1
    dp = lax.axis_size("dp")

    near, far, sq, notes = pl.pallas_call(
        functools.partial(first_kernel, taps // BLOCK),
        out_shape=(
            jax.ShapeDtypeStruct((2 * rows + TAIL, channels), BF16),
            jax.ShapeDtypeStruct((2 * TAIL, channels), BF16),
            jax.ShapeDtypeStruct((1, rows), F32),
            jax.ShapeDtypeStruct((window + own * (taps // BLOCK) + 1, rows), F32),
        ),
        in_specs=[spec(pltpu.SMEM), spec()] + [spec(pl.ANY)] * 4,
        out_specs=(spec(pl.ANY), spec(pl.ANY), spec(), spec()),
        scratch_shapes=[
            pltpu.VMEM((rows, channels), BF16),
            pltpu.VMEM((2 * rows + TAIL, channels), BF16),
            pltpu.SemaphoreType.DMA((7,)),
        ],
        compiler_params=pltpu.CompilerParams(vmem_limit_bytes=MOST),
        name="first",
    )(lengths, reward.reshape(1, rows), query, key, value, upstream)
    near = moved_up(near, "dp", 1)
    far = moved_up(far, "dp", 2)
    sq = summed_small(sq, "fsdp")

    band, band_t = pl.pallas_call(
        band_kernel,
        out_shape=(
            jax.ShapeDtypeStruct((tiles, stack, 2 * LANES), BF16),
            jax.ShapeDtypeStruct((tiles, taps + BLOCK, stack), BF16),
        ),
        in_specs=[spec()],
        out_specs=(spec(),) * 2,
        scratch_shapes=[pltpu.VMEM((groups, 2 * LANES), F32)],
        compiler_params=pltpu.CompilerParams(vmem_limit_bytes=LIMIT),
        name="band",
    )(mr_filter.T)

    part = pl.pallas_call(
        functools.partial(main_kernel, float(channels * lax.axis_size("fsdp"))),
        out_shape=jax.ShapeDtypeStruct((24 + per_tile, channels), F32),
        in_specs=[spec()] * 11,
        out_specs=spec(),
        scratch_shapes=[
            pltpu.VMEM((beside, own * SLOT, LANES), F32),
            pltpu.VMEM((beside, window * SLOT, LANES), F32),
            pltpu.VMEM((beside, window * SLOT, LANES), F32),
            pltpu.VMEM((beside, window * BLOCK, LANES), F32),
            pltpu.VMEM((beside, window * BLOCK, LANES), F32),
            pltpu.VMEM((beside, (own - 1) * BLOCK + 2 * LANES, LANES), BF16),
            pltpu.VMEM((beside, own // 2, 2 * LANES, 2 * LANES), BF16),
            pltpu.VMEM((beside, own // 2, stack, 2 * LANES), BF16),
            pltpu.VMEM((beside, window * BLOCK, LANES), F32),
            pltpu.VMEM((beside, rows, LANES), F32),
            pltpu.VMEM((tiles, per_tile * 8, 2 * LANES), F32),
            pltpu.VMEM((rows, LANES), F32),
        ],
        compiler_params=pltpu.CompilerParams(vmem_limit_bytes=LIMIT),
        name="main",
    )(
        query,
        key,
        value,
        upstream,
        near,
        far,
        sq,
        notes,
        se_filter,
        band,
        band_t,
    )

    parts = spread(part, "dp")
    grad_se, grad_mr = pl.pallas_call(
        functools.partial(last_kernel, 1.0 / rows),
        out_shape=(
            jax.ShapeDtypeStruct((3, tap_count, channels), F32),
            jax.ShapeDtypeStruct((groups, taps), F32),
        ),
        in_specs=[spec()] * len(parts),
        out_specs=(spec(),) * 2,
        compiler_params=pltpu.CompilerParams(vmem_limit_bytes=LIMIT),
        name="last",
    )(*parts)
    return grad_se, grad_mr.T


def solution(mesh):
    in_specs = (
        P("dp", "fsdp"),
        P("dp", "fsdp"),
        P("dp", "fsdp"),
        P("dp", "fsdp"),
        P("dp"),
        P(),
        P(None, None, "fsdp"),
        P(None, "fsdp"),
    )
    out_specs = (P(None, None, "fsdp"), P(None, "fsdp"))
    return jax.shard_map(
        on_device, mesh=mesh, in_specs=in_specs, out_specs=out_specs, check_vma=False
    )
```

```python
import functools

import jax
import jax.numpy as jnp
from jax import lax
from jax.experimental import pallas as pl
from jax.experimental.pallas import tpu as pltpu
from jax.sharding import PartitionSpec as P

BLOCK = 32
LANES = 128
TAIL = 16
PRE = 8
SLOT = PRE + BLOCK
LIMIT = 24 * 1024 * 1024
MOST = 60 * 1024 * 1024
TL, BD, FW = 1.5, 1.6, 3.0
COPIES = 64
F32 = jnp.float32
BF16 = jnp.bfloat16


def spec(space=pltpu.VMEM):
    return pl.BlockSpec(memory_space=space)


def cost(micros):
    return pl.CostEstimate(flops=1, bytes_accessed=int(micros * 3.6e6), transcendentals=0)


def summed(parts):
    while len(parts) > 1:
        parts = [sum(parts[i + 1 : i + 2], parts[i]) for i in range(0, len(parts), 2)]
    return parts[0]


def dot(a, b, contract, precision=None):
    return lax.dot_general(
        a, b, ((contract[0], contract[1]), ((), ())), precision=precision, preferred_element_type=F32
    )


def doc_of(lengths_ref, block):
    count = jnp.int32(0)
    end = jnp.int32(0)
    for i in range(lengths_ref.shape[0]):
        end = end + lengths_ref[i]
        count = count + jnp.where(block >= end, 1, 0)
    return jnp.where(block >= 0, count, -1)


def first_kernel(
    span,
    lengths_ref,
    reward_ref,
    q_ref,
    k_ref,
    v_ref,
    up_ref,
    h_ref,
    se_ref,
    near_ref,
    far_ref,
    sq_ref,
    note_ref,
    h_out_ref,
    se_out_ref,
    up_here,
    here,
    lengths_here,
    reward_here,
    sems,
):
    rows, channels = k_ref.shape
    tail = pl.ds(rows - TAIL, TAIL)
    pieces = (
        (up_ref, up_here),
        (q_ref.at[tail], here.at[0]),
        (k_ref.at[tail], here.at[1]),
        (v_ref.at[tail], here.at[2]),
        (lengths_ref, lengths_here),
        (reward_ref, reward_here),
        (h_ref, h_out_ref),
        (se_ref, se_out_ref),
    )
    copies = [
        pltpu.make_async_copy(source, target, sems.at[i]) for i, (source, target) in enumerate(pieces)
    ]
    for copy in copies:
        copy.start()
    copies[0].wait()
    total = jnp.zeros((rows, LANES), F32)
    for tile in range(channels // LANES):
        part = up_here[:, tile * LANES : (tile + 1) * LANES].astype(F32)
        total = total + part * part
    sq_ref[...] = jnp.broadcast_to(jnp.sum(total.T, axis=0, keepdims=True), sq_ref.shape)
    for copy in copies[1:]:
        copy.wait()
    tails = [here[i].astype(F32)[TAIL - PRE :] for i in range(3)]
    near_ref[...] = here[0]
    far_ref[...] = jnp.concatenate(tails[1:], axis=0).astype(BF16)
    own = rows // BLOCK
    window = span + own
    first = lax.axis_index("dp") * own
    docs = [doc_of(lengths_here, first + b) for b in range(-span - 1, own)]
    notes = [(docs[b + 1] == docs[b]) & (docs[b] >= 0) for b in range(window)]
    docs = docs[1:]
    notes = notes + [docs[n + s] == docs[n + span] for n in range(own) for s in range(span)]
    for i, note in enumerate(notes):
        note_ref[i : i + 1] = jnp.full((1, rows), jnp.where(note, 1.0, 0.0).astype(F32))
    note_ref[len(notes) : len(notes) + 1] = reward_here[...].astype(F32) * 0.25


def band_kernel(h_ref, band_ref, band_t_ref, row_ref):
    groups, taps = h_ref.shape
    tiles = band_ref.shape[0]
    per_tile = groups // tiles
    width = band_ref.shape[2]
    tap = lax.broadcasted_iota(jnp.int32, (taps, width), 0)
    lane = lax.broadcasted_iota(jnp.int32, (taps, width), 1)
    flip = jnp.where(tap + lane == taps, 1.0, 0.0).astype(F32)
    row_ref[...] = dot(h_ref[...], flip.astype(BF16), ((1,), (0,)))

    def one(tile, carry):
        rows = row_ref[pl.ds(pl.multiple_of(tile * per_tile, per_tile), per_tile), :]
        parts = [
            pltpu.roll(
                jnp.broadcast_to(rows[g : g + 1], (BLOCK, width)), 0, 1, stride=1, stride_axis=0
            )
            for g in range(per_tile)
        ]
        band = jnp.concatenate(parts, axis=0)
        band_ref[tile] = band.astype(BF16)
        band_t_ref[tile] = band.T[0 : taps + BLOCK].astype(BF16)
        return carry

    lax.fori_loop(0, tiles, one, 0)


def notes_of(note_ref, own, span):
    window = own + span
    joined = [note_ref[b : b + 1, 0:LANES] for b in range(window)]
    same = [
        [note_ref[window + n * span + s : window + n * span + s + 1, 0:LANES] for s in range(span)]
        for n in range(own)
    ]
    reward = note_ref[window + own * span : window + own * span + 1]
    return joined, same, reward


def lane_picks(per_tile):
    lane_group = lax.broadcasted_iota(jnp.int32, (BLOCK, LANES), 1) // (LANES // per_tile)
    return [lane_group == g for g in range(per_tile)]


def shifted(x_ref, tile, b, j):
    at = SLOT * b + PRE - j
    return x_ref[tile, at : at + BLOCK, :]


def tile_lanes(tile):
    return pl.ds(pl.multiple_of(tile * LANES, LANES), LANES)


def in_groups(count, beside, stages):
    def some(step, carry):
        now = [step * beside + side for side in range(beside)]
        kept = [None] * beside
        for stage in stages:
            kept = [stage(tile, side, got) for side, (tile, got) in enumerate(zip(now, kept))]
        return carry

    lax.fori_loop(0, count // beside, some, 0)


def forward_kernel(
    beside,
    q_ref,
    k_ref,
    v_ref,
    up_ref,
    k_near_ref,
    v_near_ref,
    near_ref,
    far_ref,
    note_ref,
    se_ref,
    band_ref,
    xq_ref,
    xk_ref,
    xv_ref,
    ks_ref,
    vs_ref,
    zw_ref,
    uq_ref,
    um_ref,
    z_ref,
):
    rows, channels = q_ref.shape
    own = rows // BLOCK
    window = xk_ref.shape[1] // SLOT
    span = window - own
    tiles = channels // LANES
    per_tile = band_ref.shape[1] // BLOCK
    tap_count = se_ref.shape[1]
    joined, same, _ = notes_of(note_ref, own, span)
    picks = lane_picks(per_tile)
    for side in range(beside):
        z_ref[side, window * BLOCK :] = jnp.zeros((z_ref.shape[1] - window * BLOCK, LANES), BF16)

    def fill(x_ref, tile, pieces, before, first_block):
        for b, piece in enumerate(pieces):
            at = SLOT * b
            x_ref[tile, at : at + PRE] = before * joined[first_block + b]
            x_ref[tile, at + PRE : at + SLOT] = piece
            before = piece[BLOCK - PRE :]

    def short(x_ref, tile, b, taps_now):
        total = taps_now[0:1] * shifted(x_ref, tile, b, 0)
        for j in range(1, tap_count):
            total = total + taps_now[j : j + 1] * shifted(x_ref, tile, b, j)
        return total

    def filters(tile, side, _):
        at = tile_lanes(tile)
        q_taps = se_ref[0, :, at].astype(F32)
        k_taps = se_ref[1, :, at].astype(F32)
        v_taps = se_ref[2, :, at].astype(F32)

        def blocks_of(ref, start, count):
            return [
                ref[start + BLOCK * b : start + BLOCK * (b + 1), at].astype(F32) for b in range(count)
            ]

        q_before = near_ref[:, at].astype(F32)[TAIL - PRE :]
        k_before, v_before = jnp.split(far_ref[:, at].astype(F32), 2)
        k_halo = blocks_of(k_near_ref, rows - span * BLOCK, span)
        v_halo = blocks_of(v_near_ref, rows - span * BLOCK, span)
        fill(xk_ref, tile, k_halo + blocks_of(k_ref, 0, own), k_before, 0)
        fill(xv_ref, tile, v_halo + blocks_of(v_ref, 0, own), v_before, 0)
        fill(xq_ref, tile, blocks_of(q_ref, 0, own), q_before, span)
        for b in range(window):
            at_b = slice(BLOCK * b, BLOCK * (b + 1))
            ks = short(xk_ref, tile, b, k_taps)
            vs = short(xv_ref, tile, b, v_taps)
            ks_ref[tile, at_b] = ks
            vs_ref[tile, at_b] = vs
            z_ref[side, at_b] = (ks * vs).astype(BF16)
        for n in range(own):
            at_n = slice(BLOCK * n, BLOCK * (n + 1))
            uq_ref[tile, at_n] = up_ref[at_n, at].astype(F32) * short(xq_ref, tile, n, q_taps)
            lanes = slice(LANES * (n % 2), LANES * (n % 2 + 1))
            for s in range(2 * LANES // BLOCK):
                piece = z_ref[side, BLOCK * (n + s) : BLOCK * (n + s + 1)]
                if s < span:
                    piece = piece * same[n][s].astype(BF16)
                zw_ref[tile, n // 2, BLOCK * s : BLOCK * (s + 1), lanes] = piece

    def medium(tile, side, _):
        at = tile_lanes(tile)
        band = band_ref[tile]
        for half in range(own // 2):
            wide = dot(band, zw_ref[tile, half], ((1,), (0,)))
            for part in range(2):
                n = 2 * half + part
                at_n = slice(BLOCK * n, BLOCK * (n + 1))
                lanes = slice(LANES * part, LANES * (part + 1))
                m = wide[0:BLOCK, lanes]
                for g in range(1, per_tile):
                    m = jnp.where(picks[g], wide[BLOCK * g : BLOCK * (g + 1), lanes], m)
                um_ref[tile, at_n] = up_ref[at_n, at].astype(F32) * m

    in_groups(tiles, beside, (filters, medium))


def backward_kernel(
    all_channels,
    beside,
    count,
    xq_ref,
    xk_ref,
    xv_ref,
    ks_ref,
    vs_ref,
    zw_ref,
    uq_ref,
    um_ref,
    note_ref,
    band_t_ref,
    *rest,
):
    *sq_refs, out_ref, dm_ref, dz_ref, skew_ref, w_ref = rest
    tiles, rows = uq_ref.shape[0:2]
    own = rows // BLOCK
    window = xk_ref.shape[1] // SLOT
    span = window - own
    per_tile = band_t_ref.shape[2] // BLOCK
    _, same, reward = notes_of(note_ref, own, span)
    masks = [jnp.where(pick, 1.0, 0.0).astype(BF16) for pick in lane_picks(per_tile)]
    weight = reward * lax.rsqrt(summed([ref[0:1] for ref in sq_refs]) / all_channels + 1e-06)
    w_ref[...] = jnp.broadcast_to(weight, (LANES, rows)).T

    def fold(x):
        return jnp.sum(x.reshape(BLOCK // 8, 8, LANES), axis=0)

    def stack(tile, side, _):
        for n in range(own):
            at_n = slice(BLOCK * n, BLOCK * (n + 1))
            dm = (w_ref[at_n] * uq_ref[tile, at_n]).astype(BF16)
            lanes = slice(LANES * (n % 2), LANES * (n % 2 + 1))
            for g in range(per_tile):
                dm_ref[side, n // 2, BLOCK * g : BLOCK * (g + 1), lanes] = dm * masks[g]

    def middle(tile, side, _):
        band_t = band_t_ref[tile]
        pair = None
        for half in range(own // 2):
            dms = dm_ref[side, half]
            back = dot(band_t, dms, ((1,), (0,)))
            both = dot(dms, zw_ref[tile, half], ((1,), (1,)))
            pair = both if pair is None else pair + both
            for part in range(2):
                n = 2 * half + part
                lanes = slice(LANES * part, LANES * (part + 1))
                for s in range(span + 1):
                    at_s = slice(BLOCK * (n + s), BLOCK * (n + s + 1))
                    term = back[BLOCK * s : BLOCK * (s + 1), lanes]
                    if s < span:
                        term = term * same[n][s]
                    if n == 0 or s == span:
                        dz_ref[side, at_s] = term
                    else:
                        dz_ref[side, at_s] += term
        lined = pair.reshape(per_tile, BLOCK // 8, 8, 2 * LANES)
        skew = None
        for r in range(BLOCK // 8):
            rows_r = lined[:, r].reshape(per_tile * 8, 2 * LANES)
            moved = pltpu.roll(rows_r, 2 * LANES - 1 - 8 * r, 1)
            skew = moved if skew is None else skew + moved
        skew_ref[tile] = skew

    def grads(tile, side, _):
        at = tile_lanes(tile)
        gq, gk, gv = ([jnp.zeros((8, LANES), F32) for _ in range(count)] for _ in range(3))
        for n in range(own):
            at_n = slice(BLOCK * n, BLOCK * (n + 1))
            cot_q = w_ref[at_n] * um_ref[tile, at_n]
            for j in range(count):
                gq[j] = gq[j] + fold(cot_q * shifted(xq_ref, tile, n, j))
        for b in range(window):
            at_b = slice(BLOCK * b, BLOCK * (b + 1))
            dz = dz_ref[side, at_b]
            cot_k = dz * vs_ref[tile, at_b]
            cot_v = dz * ks_ref[tile, at_b]
            for j in range(count):
                gk[j] = gk[j] + fold(cot_k * shifted(xk_ref, tile, b, j))
                gv[j] = gv[j] + fold(cot_v * shifted(xv_ref, tile, b, j))
        for i, sums in enumerate((gq, gk, gv)):
            for j in range(count):
                out_ref[8 * i + j : 8 * i + j + 1, at] = jnp.sum(sums[j], axis=0, keepdims=True)
            out_ref[8 * i + count : 8 * i + 8, at] = jnp.zeros((8 - count, LANES), F32)

    in_groups(tiles, beside, (stack, middle, grads))
    skew = skew_ref[...].reshape(tiles * per_tile * 8, 2 * LANES)
    row_index = lax.broadcasted_iota(jnp.int32, skew.shape, 0)
    for bit in range(3):
        moved = pltpu.roll(skew, 2 * LANES - (1 << bit), 1)
        skew = jnp.where((row_index >> bit) & 1 == 1, moved, skew)
    totals = jnp.sum(skew[:, 0:LANES].reshape(tiles * per_tile, 8, LANES), axis=1)
    for tile in range(tiles):
        out_ref[24 : 24 + per_tile, LANES * tile : LANES * (tile + 1)] = totals[
            per_tile * tile : per_tile * (tile + 1)
        ]


def last_kernel(scale, *refs):
    *part_refs, se_ref, mr_ref = refs
    total = summed([ref[...].astype(F32) for ref in part_refs]) * scale
    tap_count = se_ref.shape[1]
    channels = total.shape[1]
    for i in range(3):
        se_ref[i] = total[8 * i : 8 * i + tap_count]
    flat = jnp.concatenate(
        [total[24:, t * LANES : (t + 1) * LANES] for t in range(channels // LANES)], axis=0
    )
    tap = lax.broadcasted_iota(jnp.int32, (LANES, LANES), 0)
    lane = lax.broadcasted_iota(jnp.int32, (LANES, LANES), 1)
    flip = jnp.where(tap + lane == LANES - 1, 1.0, 0.0).astype(F32)
    mr_ref[...] = dot(flat, flip, ((1,), (0,)), lax.Precision.HIGHEST)


def swapped(value, axis, distance):
    count = lax.axis_size(axis)
    return lax.ppermute(value, axis, [(i, i ^ distance) for i in range(count)])


def summed_small(value, axis, beside):
    count = lax.axis_size(axis)
    if count & (count - 1):
        return [lax.psum(value, axis)], beside
    distance = 1
    while 2 * distance < count:
        got = swapped(value, axis, distance)
        if distance == 1:
            got, beside = lax.optimization_barrier((got, beside))
        value = value + got
        distance *= 2
    return [value, swapped(value, axis, distance)], beside


def spread(part, axis):
    count = lax.axis_size(axis)
    if count & (count - 1) or count < 8:
        return [lax.psum(part, axis)]
    mine = (part + swapped(part, axis, 1)).astype(BF16)
    distance = 8
    while distance < count:
        mine = (mine.astype(F32) + swapped(mine, axis, distance).astype(F32)).astype(BF16)
        distance *= 2
    return [mine] + [swapped(mine, axis, d) for d in (2, 4, 6)]


def moved_up(value, axis, steps):
    count = lax.axis_size(axis)
    return lax.ppermute(value, axis, [(i, (i + steps) % count) for i in range(count)])


def on_device(query, key, value, upstream, reward, lengths, se_filter, mr_filter):
    rows, channels = query.shape
    taps, groups = mr_filter.shape
    tap_count = se_filter.shape[1]
    tiles = channels // LANES
    per_tile = groups // tiles
    stack = per_tile * BLOCK
    own = rows // BLOCK
    span = taps // BLOCK
    window = own + span
    beside = 2 if tiles % 2 == 0 else 1
    dp = lax.axis_size("dp")

    k_near = moved_up(key, "dp", 1)
    v_near = moved_up(value, "dp", 1)
    near, far, sq, notes, medium_taps, short_taps = pl.pallas_call(
        functools.partial(first_kernel, span),
        out_shape=(
            jax.ShapeDtypeStruct((TAIL, channels), BF16),
            jax.ShapeDtypeStruct((2 * PRE, channels), BF16),
            jax.ShapeDtypeStruct((COPIES, rows), F32),
            jax.ShapeDtypeStruct((window + own * span + 1, rows), F32),
            jax.ShapeDtypeStruct((groups, taps), BF16),
            jax.ShapeDtypeStruct(se_filter.shape, BF16),
        ),
        in_specs=[spec(pl.ANY)] * 8,
        out_specs=(spec(),) * 6,
        scratch_shapes=[
            pltpu.VMEM((rows, channels), BF16),
            pltpu.VMEM((3, TAIL, channels), BF16),
            pltpu.SMEM(lengths.shape, jnp.int32),
            pltpu.VMEM((1, rows), jnp.int32),
            pltpu.SemaphoreType.DMA((8,)),
        ],
        compiler_params=pltpu.CompilerParams(vmem_limit_bytes=LIMIT),
        cost_estimate=cost(TL),
        name="first",
    )(
        *[
            pltpu.with_memory_space_constraint(x, pltpu.HBM)
            for x in (
                lengths,
                reward.reshape(1, rows),
                query,
                key,
                value,
                upstream,
                mr_filter.T,
                se_filter,
            )
        ]
    )
    near = moved_up(near, "dp", 1)
    far = moved_up(far, "dp", 2)

    band, band_t = pl.pallas_call(
        band_kernel,
        out_shape=(
            jax.ShapeDtypeStruct((tiles, stack, 2 * LANES), BF16),
            jax.ShapeDtypeStruct((tiles, taps + BLOCK, stack), BF16),
        ),
        in_specs=[spec()],
        out_specs=(spec(),) * 2,
        scratch_shapes=[pltpu.VMEM((groups, 2 * LANES), F32)],
        compiler_params=pltpu.CompilerParams(vmem_limit_bytes=LIMIT),
        cost_estimate=cost(BD),
        name="band",
    )(medium_taps)

    squares, (band, band_t) = summed_small(sq, "fsdp", (band, band_t))
    kept = pl.pallas_call(
        functools.partial(forward_kernel, beside),
        out_shape=(
            jax.ShapeDtypeStruct((tiles, own * SLOT, LANES), F32),
            jax.ShapeDtypeStruct((tiles, window * SLOT, LANES), F32),
            jax.ShapeDtypeStruct((tiles, window * SLOT, LANES), F32),
            jax.ShapeDtypeStruct((tiles, window * BLOCK, LANES), F32),
            jax.ShapeDtypeStruct((tiles, window * BLOCK, LANES), F32),
            jax.ShapeDtypeStruct((tiles, own // 2, 2 * LANES, 2 * LANES), BF16),
            jax.ShapeDtypeStruct((tiles, rows, LANES), F32),
            jax.ShapeDtypeStruct((tiles, rows, LANES), F32),
        ),
        in_specs=[spec()] * 11,
        out_specs=(spec(),) * 8,
        scratch_shapes=[pltpu.VMEM((beside, (own - 1) * BLOCK + 2 * LANES, LANES), BF16)],
        compiler_params=pltpu.CompilerParams(vmem_limit_bytes=LIMIT),
        cost_estimate=cost(FW),
        name="forward",
    )(query, key, value, upstream, k_near, v_near, near, far, notes, short_taps, band)
    part = pl.pallas_call(
        functools.partial(
            backward_kernel, float(channels * lax.axis_size("fsdp")), beside, tap_count
        ),
        out_shape=jax.ShapeDtypeStruct((24 + per_tile, channels), F32),
        in_specs=[spec()] * (10 + len(squares)),
        out_specs=spec(),
        scratch_shapes=[
            pltpu.VMEM((beside, own // 2, stack, 2 * LANES), BF16),
            pltpu.VMEM((beside, window * BLOCK, LANES), F32),
            pltpu.VMEM((tiles, per_tile * 8, 2 * LANES), F32),
            pltpu.VMEM((rows, LANES), F32),
        ],
        compiler_params=pltpu.CompilerParams(vmem_limit_bytes=LIMIT),
        name="backward",
    )(*kept, notes, band_t, *squares)

    parts = spread(part, "dp")
    grad_se, grad_mr = pl.pallas_call(
        functools.partial(last_kernel, 1.0 / rows),
        out_shape=(
            jax.ShapeDtypeStruct((3, tap_count, channels), F32),
            jax.ShapeDtypeStruct((groups, taps), F32),
        ),
        in_specs=[spec()] * len(parts),
        out_specs=(spec(),) * 2,
        compiler_params=pltpu.CompilerParams(vmem_limit_bytes=LIMIT),
        name="last",
    )(*parts)
    return grad_se, grad_mr.T


def solution(mesh):
    in_specs = (
        P("dp", "fsdp"),
        P("dp", "fsdp"),
        P("dp", "fsdp"),
        P("dp", "fsdp"),
        P("dp"),
        P(),
        P(None, None, "fsdp"),
        P(None, "fsdp"),
    )
    out_specs = (P(None, None, "fsdp"), P(None, "fsdp"))
    return jax.shard_map(
        on_device, mesh=mesh, in_specs=in_specs, out_specs=out_specs, check_vma=False
    )
```

```python
import functools
import math

import jax
import jax.numpy as jnp
from jax import lax
from jax.experimental import pallas as pl
from jax.experimental.pallas import tpu as pltpu
from jax.sharding import PartitionSpec as P

BLOCK = 32
LANES = 128
TAIL = 16
PRE = 8
SLOT = PRE + BLOCK
LIMIT = 24 * 1024 * 1024
COPIES = 64
F32 = jnp.float32
BF16 = jnp.bfloat16


def spec(space=pltpu.VMEM):
    return pl.BlockSpec(memory_space=space)


def cost(micros):
    return pl.CostEstimate(flops=1, bytes_accessed=int(micros * 3.6e6), transcendentals=0)


def summed(parts):
    while len(parts) > 1:
        parts = [sum(parts[i + 1 : i + 2], parts[i]) for i in range(0, len(parts), 2)]
    return parts[0]


def dot(a, b, contract, precision=None):
    return lax.dot_general(
        a, b, ((contract[0], contract[1]), ((), ())), precision=precision, preferred_element_type=F32
    )


def doc_of(lengths_ref, block):
    count = jnp.int32(0)
    end = jnp.int32(0)
    for i in range(lengths_ref.shape[0]):
        end = end + lengths_ref[i]
        count = count + jnp.where(block >= end, 1, 0)
    return jnp.where(block >= 0, count, -1)


def first_kernel(
    span,
    lengths_ref,
    reward_ref,
    q_ref,
    k_ref,
    v_ref,
    up_ref,
    h_ref,
    se_ref,
    near_ref,
    far_ref,
    sq_ref,
    note_ref,
    h_out_ref,
    se_out_ref,
    up_here,
    k_here,
    lengths_here,
    reward_here,
    sems,
):
    rows, channels = k_ref.shape
    tail = pl.ds(rows - TAIL, TAIL)
    pieces = (
        (up_ref, up_here),
        (v_ref, near_ref.at[pl.ds(0, rows)]),
        (q_ref.at[tail], near_ref.at[pl.ds(rows, TAIL)]),
        (k_ref.at[tail], k_here),
        (lengths_ref, lengths_here),
        (reward_ref, reward_here),
        (h_ref, h_out_ref),
        (se_ref, se_out_ref),
    )
    copies = [
        pltpu.make_async_copy(source, target, sems.at[i]) for i, (source, target) in enumerate(pieces)
    ]
    for copy in copies:
        copy.start()
    copies[4].wait()
    copies[5].wait()
    own = rows // BLOCK
    window = span + own
    first = lax.axis_index("dp") * own
    docs = [doc_of(lengths_here, first + b) for b in range(-span - 1, own)]
    notes = [(docs[b + 1] == docs[b]) & (docs[b] >= 0) for b in range(window)]
    docs = docs[1:]
    notes = notes + [docs[n + s] == docs[n + span] for n in range(own) for s in range(span)]
    for i, note in enumerate(notes):
        note_ref[i : i + 1] = jnp.full((1, rows), jnp.where(note, 1.0, 0.0).astype(F32))
    note_ref[len(notes) : len(notes) + 1] = reward_here[...].astype(F32) * 0.25
    copies[0].wait()
    total = jnp.zeros((rows, LANES), F32)
    for tile in range(channels // LANES):
        part = up_here[:, tile * LANES : (tile + 1) * LANES].astype(F32)
        total = total + part * part
    sq_ref[...] = jnp.broadcast_to(jnp.sum(total.T, axis=0, keepdims=True), sq_ref.shape)
    for copy in copies[1:4] + copies[6:]:
        copy.wait()
    tails = [ref[...].astype(F32)[TAIL - PRE :] for ref in (k_here, near_ref.at[tail])]
    far_ref[...] = jnp.concatenate(tails, axis=0).astype(BF16)


def band_kernel(h_ref, band_ref, band_t_ref, row_ref):
    groups, taps = h_ref.shape
    tiles = band_ref.shape[0]
    per_tile = groups // tiles
    width = band_ref.shape[2]
    tap = lax.broadcasted_iota(jnp.int32, (taps, width), 0)
    lane = lax.broadcasted_iota(jnp.int32, (taps, width), 1)
    flip = jnp.where(tap + lane == taps, 1.0, 0.0).astype(F32)
    row_ref[...] = dot(h_ref[...], flip.astype(BF16), ((1,), (0,)))

    for tile in range(tiles):
        rows = row_ref[tile * per_tile : (tile + 1) * per_tile]
        parts = [
            pltpu.roll(
                jnp.broadcast_to(rows[g : g + 1], (BLOCK, width)), 0, 1, stride=1, stride_axis=0
            )
            for g in range(per_tile)
        ]
        band = jnp.concatenate(parts, axis=0)
        band_ref[tile] = band.astype(BF16)
        band_t_ref[tile] = band.astype(BF16).T[0 : taps + BLOCK]


def notes_of(note_ref, own, span):
    window = own + span
    joined = [note_ref[b : b + 1, 0:LANES] for b in range(window)]
    same = [
        [note_ref[window + n * span + s : window + n * span + s + 1, 0:LANES] for s in range(span)]
        for n in range(own)
    ]
    reward = note_ref[window + own * span : window + own * span + 1]
    return joined, same, reward


def lane_picks(per_tile):
    lane_group = lax.broadcasted_iota(jnp.int32, (BLOCK, LANES), 1) // (LANES // per_tile)
    return [lane_group == g for g in range(per_tile)]


def shifted(x_ref, tile, b, j):
    at = SLOT * b + PRE - j
    return x_ref[tile, at : at + BLOCK, :]


def tile_lanes(tile):
    return pl.ds(pl.multiple_of(tile * LANES, LANES), LANES)


def in_groups(count, beside, stages):
    def some(step, carry):
        now = [step * beside + side for side in range(beside)]
        kept = [None] * beside
        for stage in stages:
            kept = [stage(tile, side, got) for side, (tile, got) in enumerate(zip(now, kept))]
        return carry

    lax.fori_loop(0, count // beside, some, 0)


def blocks_of(ref, at, start, count):
    return [ref[start + BLOCK * b : start + BLOCK * (b + 1), at].astype(F32) for b in range(count)]


def fill(x_ref, tile, pieces, before, joined):
    for b, piece in enumerate(pieces):
        at = SLOT * b
        x_ref[tile, at : at + PRE] = before * joined[b]
        x_ref[tile, at + PRE : at + SLOT] = piece
        before = piece[BLOCK - PRE :]


def short(x_ref, tile, b, taps_now):
    total = taps_now[0:1] * shifted(x_ref, tile, b, 0)
    for j in range(1, taps_now.shape[0]):
        total = total + taps_now[j : j + 1] * shifted(x_ref, tile, b, j)
    return total


def key_kernel(beside, k_ref, k_near_ref, note_ref, se_ref, xk_ref, ks_ref):
    rows, channels = k_ref.shape
    own = rows // BLOCK
    later = xk_ref.shape[1] // SLOT
    span = later + 1 - own
    joined, _, _ = notes_of(note_ref, own, span)

    def filters(tile, side, _):
        at = tile_lanes(tile)
        k_taps = se_ref[1, :, at].astype(F32)
        halo = blocks_of(k_near_ref, at, rows - span * BLOCK, span)
        before = halo[0][BLOCK - PRE :]
        fill(xk_ref, tile, halo[1:] + blocks_of(k_ref, at, 0, own), before, joined[1:])
        for b in range(later):
            ks_ref[tile, BLOCK * b : BLOCK * (b + 1)] = short(xk_ref, tile, b, k_taps)

    in_groups(channels // LANES, beside, (filters,))


def forward_kernel(
    beside,
    q_ref,
    v_ref,
    up_ref,
    k_near_ref,
    near_ref,
    far_ref,
    note_ref,
    se_ref,
    band_ref,
    ks_ref,
    xq_ref,
    xk_ref,
    xv_ref,
    ks_first_ref,
    vs_ref,
    zw_ref,
    uq_ref,
    um_ref,
    z_ref,
):
    rows, channels = q_ref.shape
    own = rows // BLOCK
    window = xv_ref.shape[1] // SLOT
    span = window - own
    tiles = channels // LANES
    per_tile = band_ref.shape[1] // BLOCK
    joined, same, _ = notes_of(note_ref, own, span)
    picks = lane_picks(per_tile)
    for side in range(beside):
        z_ref[side, window * BLOCK :] = jnp.zeros((z_ref.shape[1] - window * BLOCK, LANES), BF16)

    def filters(tile, side, _):
        at = tile_lanes(tile)
        q_taps, k_taps, v_taps = (se_ref[i, :, at].astype(F32) for i in range(3))
        q_before = near_ref[rows:, at].astype(F32)[TAIL - PRE :]
        k_before, v_before = jnp.split(far_ref[:, at].astype(F32), 2)
        v_halo = blocks_of(near_ref, at, rows - span * BLOCK, span)
        fill(xv_ref, tile, v_halo + blocks_of(v_ref, at, 0, own), v_before, joined)
        fill(xk_ref, tile, blocks_of(k_near_ref, at, rows - span * BLOCK, 1), k_before, joined)
        fill(xq_ref, tile, blocks_of(q_ref, at, 0, own), q_before, joined[span:])
        for b in range(window):
            at_b = slice(BLOCK * b, BLOCK * (b + 1))
            vs = short(xv_ref, tile, b, v_taps)
            vs_ref[tile, at_b] = vs
            if b == 0:
                ks = short(xk_ref, tile, b, k_taps)
                ks_first_ref[tile] = ks
            else:
                ks = ks_ref[tile, BLOCK * (b - 1) : BLOCK * b]
            z_ref[side, at_b] = (ks * vs).astype(BF16)
        for n in range(own):
            at_n = slice(BLOCK * n, BLOCK * (n + 1))
            uq_ref[tile, at_n] = up_ref[at_n, at].astype(F32) * short(xq_ref, tile, n, q_taps)
            lanes = slice(LANES * (n % 2), LANES * (n % 2 + 1))
            for s in range(2 * LANES // BLOCK):
                piece = z_ref[side, BLOCK * (n + s) : BLOCK * (n + s + 1)]
                if s < span:
                    piece = piece * same[n][s].astype(BF16)
                zw_ref[tile, n // 2, BLOCK * s : BLOCK * (s + 1), lanes] = piece

    def medium(tile, side, _):
        at = tile_lanes(tile)
        band = band_ref[tile]
        for half in range(own // 2):
            wide = dot(band, zw_ref[tile, half], ((1,), (0,)))
            for part in range(2):
                n = 2 * half + part
                at_n = slice(BLOCK * n, BLOCK * (n + 1))
                lanes = slice(LANES * part, LANES * (part + 1))
                m = wide[0:BLOCK, lanes]
                for g in range(1, per_tile):
                    m = jnp.where(picks[g], wide[BLOCK * g : BLOCK * (g + 1), lanes], m)
                um_ref[tile, at_n] = up_ref[at_n, at].astype(F32) * m

    in_groups(tiles, beside, (filters, medium))


def backward_kernel(
    all_channels,
    beside,
    count,
    xk_ref,
    ks_ref,
    xq_ref,
    xk_first_ref,
    xv_ref,
    ks_first_ref,
    vs_ref,
    zw_ref,
    uq_ref,
    um_ref,
    note_ref,
    band_t_ref,
    *rest,
):
    *sq_refs, out_ref, dm_ref, dz_ref, skew_ref, w_ref = rest
    tiles, rows = uq_ref.shape[0:2]
    own = rows // BLOCK
    window = xv_ref.shape[1] // SLOT
    span = window - own
    per_tile = band_t_ref.shape[2] // BLOCK
    _, same, reward = notes_of(note_ref, own, span)
    masks = [jnp.where(pick, 1.0, 0.0).astype(BF16) for pick in lane_picks(per_tile)]
    weight = reward * lax.rsqrt(summed([ref[0:1] for ref in sq_refs]) / all_channels + 1e-06)
    w_ref[...] = jnp.broadcast_to(weight, (LANES, rows)).T

    def fold(x):
        return jnp.sum(x.reshape(BLOCK // 8, 8, LANES), axis=0)

    def stack(tile, side, _):
        for n in range(own):
            at_n = slice(BLOCK * n, BLOCK * (n + 1))
            dm = (w_ref[at_n] * uq_ref[tile, at_n]).astype(BF16)
            lanes = slice(LANES * (n % 2), LANES * (n % 2 + 1))
            for g in range(per_tile):
                dm_ref[side, n // 2, BLOCK * g : BLOCK * (g + 1), lanes] = dm * masks[g]

    def middle(tile, side, _):
        band_t = band_t_ref[tile]
        pair = None
        for half in range(own // 2):
            dms = dm_ref[side, half]
            back = dot(band_t, dms, ((1,), (0,)))
            both = dot(dms, zw_ref[tile, half], ((1,), (1,)))
            pair = both if pair is None else pair + both
            for part in range(2):
                n = 2 * half + part
                lanes = slice(LANES * part, LANES * (part + 1))
                for s in range(span + 1):
                    at_s = slice(BLOCK * (n + s), BLOCK * (n + s + 1))
                    term = back[BLOCK * s : BLOCK * (s + 1), lanes]
                    if s < span:
                        term = term * same[n][s]
                    if n == 0 or s == span:
                        dz_ref[side, at_s] = term
                    else:
                        dz_ref[side, at_s] += term
        lined = pair.reshape(per_tile, BLOCK // 8, 8, 2 * LANES)
        skew = None
        for r in range(BLOCK // 8):
            rows_r = lined[:, r].reshape(per_tile * 8, 2 * LANES)
            moved = pltpu.roll(rows_r, 2 * LANES - 1 - 8 * r, 1)
            skew = moved if skew is None else skew + moved
        skew_ref[tile] = skew

    def grads(tile, side, _):
        at = tile_lanes(tile)
        gq, gk, gv = ([jnp.zeros((8, LANES), F32) for _ in range(count)] for _ in range(3))
        for n in range(own):
            at_n = slice(BLOCK * n, BLOCK * (n + 1))
            cot_q = w_ref[at_n] * um_ref[tile, at_n]
            for j in range(count):
                gq[j] = gq[j] + fold(cot_q * shifted(xq_ref, tile, n, j))
        for b in range(window):
            at_b = slice(BLOCK * b, BLOCK * (b + 1))
            dz = dz_ref[side, at_b]
            cot_k = dz * vs_ref[tile, at_b]
            ks = ks_ref[tile, BLOCK * (b - 1) : BLOCK * b] if b else ks_first_ref[tile]
            cot_v = dz * ks
            for j in range(count):
                k_rows = shifted(xk_ref, tile, b - 1, j) if b else shifted(xk_first_ref, tile, 0, j)
                gk[j] = gk[j] + fold(cot_k * k_rows)
                gv[j] = gv[j] + fold(cot_v * shifted(xv_ref, tile, b, j))
        for i, sums in enumerate((gq, gk, gv)):
            for j in range(count):
                out_ref[8 * i + j : 8 * i + j + 1, at] = jnp.sum(sums[j], axis=0, keepdims=True)
            out_ref[8 * i + count : 8 * i + 8, at] = jnp.zeros((8 - count, LANES), F32)

    in_groups(tiles, beside, (stack, middle, grads))
    skew = skew_ref[...].reshape(tiles * per_tile * 8, 2 * LANES)
    row_index = lax.broadcasted_iota(jnp.int32, skew.shape, 0)
    for bit in range(3):
        moved = pltpu.roll(skew, 2 * LANES - (1 << bit), 1)
        skew = jnp.where((row_index >> bit) & 1 == 1, moved, skew)
    totals = jnp.sum(skew[:, 0:LANES].reshape(tiles * per_tile, 8, LANES), axis=1)
    for tile in range(tiles):
        out_ref[24 : 24 + per_tile, LANES * tile : LANES * (tile + 1)] = totals[
            per_tile * tile : per_tile * (tile + 1)
        ]


def last_kernel(scale, *refs):
    *part_refs, se_ref, mr_ref = refs
    total = summed([ref[...].astype(F32) for ref in part_refs]) * scale
    tap_count = se_ref.shape[1]
    channels = total.shape[1]
    for i in range(3):
        se_ref[i] = total[8 * i : 8 * i + tap_count]
    flat = jnp.concatenate(
        [total[24:, t * LANES : (t + 1) * LANES] for t in range(channels // LANES)], axis=0
    )
    tap = lax.broadcasted_iota(jnp.int32, (LANES, LANES), 0)
    lane = lax.broadcasted_iota(jnp.int32, (LANES, LANES), 1)
    flip = jnp.where(tap + lane == LANES - 1, 1.0, 0.0).astype(F32)
    mr_ref[...] = dot(flat, flip, ((1,), (0,)), lax.Precision.HIGHEST)


def swapped(value, axis, distance):
    count = lax.axis_size(axis)
    return lax.ppermute(value, axis, [(i, i ^ distance) for i in range(count)])


def summed_small(value, axis, beside):
    count = lax.axis_size(axis)
    if count & (count - 1):
        return [lax.psum(value, axis)], beside
    distance = 1
    while 2 * distance < count:
        got = swapped(value, axis, distance)
        if distance == 1:
            got, beside = lax.optimization_barrier((got, beside))
        value = value + got
        distance *= 2
    return [value, swapped(value, axis, distance)], beside


def spread(part, axis):
    count = lax.axis_size(axis)
    if count & (count - 1) or count < 8:
        return [lax.psum(part, axis)]
    mine = (part + swapped(part, axis, 1)).astype(BF16)
    distance = 8
    while distance < count:
        mine = (mine.astype(F32) + swapped(mine, axis, distance).astype(F32)).astype(BF16)
        distance *= 2
    return [mine] + [swapped(mine, axis, d) for d in (2, 4, 6)]


def moved_up(value, axis, steps):
    count = lax.axis_size(axis)
    return lax.ppermute(value, axis, [(i, (i + steps) % count) for i in range(count)])


def on_device(query, key, value, upstream, reward, lengths, se_filter, mr_filter):
    rows, channels = query.shape
    taps, groups = mr_filter.shape
    tap_count = se_filter.shape[1]
    tiles = channels // LANES
    per_tile = groups // tiles
    stack = per_tile * BLOCK
    own = rows // BLOCK
    span = taps // BLOCK
    window = own + span
    beside = math.gcd(tiles, 8)
    dp = lax.axis_size("dp")

    k_near = moved_up(key, "dp", 1)
    near, far, sq, notes, medium_taps, short_taps = pl.pallas_call(
        functools.partial(first_kernel, span),
        out_shape=(
            jax.ShapeDtypeStruct((rows + TAIL, channels), BF16),
            jax.ShapeDtypeStruct((2 * PRE, channels), BF16),
            jax.ShapeDtypeStruct((COPIES, rows), F32),
            jax.ShapeDtypeStruct((window + own * span + 1, rows), F32),
            jax.ShapeDtypeStruct((groups, taps), BF16),
            jax.ShapeDtypeStruct(se_filter.shape, BF16),
        ),
        in_specs=[spec(pl.ANY)] * 8,
        out_specs=(spec(),) * 6,
        scratch_shapes=[
            pltpu.VMEM((rows, channels), BF16),
            pltpu.VMEM((TAIL, channels), BF16),
            pltpu.SMEM(lengths.shape, jnp.int32),
            pltpu.VMEM((1, rows), jnp.int32),
            pltpu.SemaphoreType.DMA((8,)),
        ],
        compiler_params=pltpu.CompilerParams(vmem_limit_bytes=LIMIT),
        cost_estimate=cost(1.2),
        name="first",
    )(
        *[
            pltpu.with_memory_space_constraint(x, pltpu.HBM)
            for x in (
                lengths,
                reward.reshape(1, rows),
                query,
                key,
                value,
                upstream,
                mr_filter.T,
                se_filter,
            )
        ]
    )
    near = moved_up(near, "dp", 1)
    far = moved_up(far, "dp", 2)

    band, band_t = pl.pallas_call(
        band_kernel,
        out_shape=(
            jax.ShapeDtypeStruct((tiles, stack, 2 * LANES), BF16),
            jax.ShapeDtypeStruct((tiles, taps + BLOCK, stack), BF16),
        ),
        in_specs=[spec()],
        out_specs=(spec(),) * 2,
        scratch_shapes=[pltpu.VMEM((groups, 2 * LANES), F32)],
        compiler_params=pltpu.CompilerParams(vmem_limit_bytes=LIMIT),
        cost_estimate=cost(1.0),
        name="band",
    )(medium_taps)

    keys = pl.pallas_call(
        functools.partial(key_kernel, beside),
        out_shape=(
            jax.ShapeDtypeStruct((tiles, (window - 1) * SLOT, LANES), F32),
            jax.ShapeDtypeStruct((tiles, (window - 1) * BLOCK, LANES), F32),
        ),
        in_specs=[spec()] * 4,
        out_specs=(spec(),) * 2,
        compiler_params=pltpu.CompilerParams(vmem_limit_bytes=LIMIT),
        cost_estimate=cost(0.5),
        name="keys",
    )(key, k_near, notes, short_taps)
    squares, (band, band_t, keys) = summed_small(sq, "fsdp", (band, band_t, keys))
    kept = pl.pallas_call(
        functools.partial(forward_kernel, beside),
        out_shape=(
            jax.ShapeDtypeStruct((tiles, own * SLOT, LANES), F32),
            jax.ShapeDtypeStruct((tiles, SLOT, LANES), F32),
            jax.ShapeDtypeStruct((tiles, window * SLOT, LANES), F32),
            jax.ShapeDtypeStruct((tiles, BLOCK, LANES), F32),
            jax.ShapeDtypeStruct((tiles, window * BLOCK, LANES), F32),
            jax.ShapeDtypeStruct((tiles, own // 2, 2 * LANES, 2 * LANES), BF16),
            jax.ShapeDtypeStruct((tiles, rows, LANES), F32),
            jax.ShapeDtypeStruct((tiles, rows, LANES), F32),
        ),
        in_specs=[spec()] * 10,
        out_specs=(spec(),) * 8,
        scratch_shapes=[pltpu.VMEM((beside, (own - 1) * BLOCK + 2 * LANES, LANES), BF16)],
        compiler_params=pltpu.CompilerParams(vmem_limit_bytes=LIMIT),
        cost_estimate=cost(2.0),
        name="forward",
    )(query, value, upstream, k_near, near, far, notes, short_taps, band, keys[1])
    part = pl.pallas_call(
        functools.partial(
            backward_kernel, float(channels * lax.axis_size("fsdp")), beside, tap_count
        ),
        out_shape=jax.ShapeDtypeStruct((24 + per_tile, channels), F32),
        in_specs=[spec()] * (12 + len(squares)),
        out_specs=spec(),
        scratch_shapes=[
            pltpu.VMEM((beside, own // 2, stack, 2 * LANES), BF16),
            pltpu.VMEM((beside, window * BLOCK, LANES), F32),
            pltpu.VMEM((tiles, per_tile * 8, 2 * LANES), F32),
            pltpu.VMEM((rows, LANES), F32),
        ],
        compiler_params=pltpu.CompilerParams(vmem_limit_bytes=LIMIT),
        name="backward",
    )(*keys, *kept, notes, band_t, *squares)

    parts = spread(part, "dp")
    grad_se, grad_mr = pl.pallas_call(
        functools.partial(last_kernel, 1.0 / rows),
        out_shape=(
            jax.ShapeDtypeStruct((3, tap_count, channels), F32),
            jax.ShapeDtypeStruct((groups, taps), F32),
        ),
        in_specs=[spec()] * len(parts),
        out_specs=(spec(),) * 2,
        compiler_params=pltpu.CompilerParams(vmem_limit_bytes=LIMIT),
        name="last",
    )(*parts)
    return grad_se, grad_mr.T


def solution(mesh):
    in_specs = (
        P("dp", "fsdp"),
        P("dp", "fsdp"),
        P("dp", "fsdp"),
        P("dp", "fsdp"),
        P("dp"),
        P(),
        P(None, None, "fsdp"),
        P(None, "fsdp"),
    )
    out_specs = (P(None, None, "fsdp"), P(None, "fsdp"))
    return jax.shard_map(
        on_device, mesh=mesh, in_specs=in_specs, out_specs=out_specs, check_vma=False
    )
```

```python
import functools
import math

import jax
import jax.numpy as jnp
from jax import lax
from jax.experimental import pallas as pl
from jax.experimental.pallas import tpu as pltpu
from jax.sharding import PartitionSpec as P

BLOCK = 32
LANES = 128
TAIL = 16
PRE = 8
SLOT = PRE + BLOCK
LIMIT = 24 * 1024 * 1024
COPIES = 64
F32 = jnp.float32
BF16 = jnp.bfloat16


def spec(space=pltpu.VMEM):
    return pl.BlockSpec(memory_space=space)


def cost(micros):
    return pl.CostEstimate(flops=1, bytes_accessed=int(micros * 3.6e6), transcendentals=0)


def summed(parts):
    while len(parts) > 1:
        parts = [sum(parts[i + 1 : i + 2], parts[i]) for i in range(0, len(parts), 2)]
    return parts[0]


def dot(a, b, contract, precision=None):
    return lax.dot_general(
        a, b, ((contract[0], contract[1]), ((), ())), precision=precision, preferred_element_type=F32
    )


def doc_of(lengths_ref, block):
    count = jnp.int32(0)
    end = jnp.int32(0)
    for i in range(lengths_ref.shape[0]):
        end = end + lengths_ref[i]
        count = count + jnp.where(block >= end, 1, 0)
    return jnp.where(block >= 0, count, -1)


def first_kernel(
    span,
    lengths_ref,
    reward_ref,
    q_ref,
    k_ref,
    v_ref,
    up_ref,
    h_ref,
    se_ref,
    near_ref,
    far_ref,
    sq_ref,
    note_ref,
    h_out_ref,
    se_out_ref,
    up_here,
    k_here,
    lengths_here,
    reward_here,
    sems,
):
    rows, channels = k_ref.shape
    tail = pl.ds(rows - TAIL, TAIL)
    pieces = (
        (up_ref, up_here),
        (v_ref, near_ref.at[pl.ds(0, rows)]),
        (q_ref.at[tail], near_ref.at[pl.ds(rows, TAIL)]),
        (k_ref.at[tail], k_here),
        (lengths_ref, lengths_here),
        (reward_ref, reward_here),
        (h_ref, h_out_ref),
        (se_ref, se_out_ref),
    )
    copies = [
        pltpu.make_async_copy(source, target, sems.at[i]) for i, (source, target) in enumerate(pieces)
    ]
    for copy in copies:
        copy.start()
    copies[4].wait()
    copies[5].wait()
    own = rows // BLOCK
    window = span + own
    first = lax.axis_index("dp") * own
    docs = [doc_of(lengths_here, first + b) for b in range(-span - 1, own)]
    notes = [(docs[b + 1] == docs[b]) & (docs[b] >= 0) for b in range(window)]
    docs = docs[1:]
    notes = notes + [docs[n + s] == docs[n + span] for n in range(own) for s in range(span)]
    for i, note in enumerate(notes):
        note_ref[i : i + 1] = jnp.full((1, rows), jnp.where(note, 1.0, 0.0).astype(F32))
    note_ref[len(notes) : len(notes) + 1] = reward_here[...].astype(F32) * 0.25
    copies[0].wait()
    total = jnp.zeros((rows, LANES), F32)
    for tile in range(channels // LANES):
        part = up_here[:, tile * LANES : (tile + 1) * LANES].astype(F32)
        total = total + part * part
    sq_ref[...] = jnp.broadcast_to(jnp.sum(total.T, axis=0, keepdims=True), sq_ref.shape)
    for copy in copies[1:4] + copies[6:]:
        copy.wait()
    tails = [ref[...].astype(F32)[TAIL - PRE :] for ref in (k_here, near_ref.at[tail])]
    far_ref[...] = jnp.concatenate(tails, axis=0).astype(BF16)


def band_kernel(h_ref, band_ref, band_t_ref, row_ref):
    groups, taps = h_ref.shape
    tiles = band_ref.shape[0]
    per_tile = groups // tiles
    width = band_ref.shape[2]
    tap = lax.broadcasted_iota(jnp.int32, (taps, width), 0)
    lane = lax.broadcasted_iota(jnp.int32, (taps, width), 1)
    flip = jnp.where(tap + lane == taps, 1.0, 0.0).astype(F32)
    row_ref[...] = dot(h_ref[...], flip.astype(BF16), ((1,), (0,)))

    for tile in range(tiles):
        rows = row_ref[tile * per_tile : (tile + 1) * per_tile]
        parts = [
            pltpu.roll(
                jnp.broadcast_to(rows[g : g + 1], (BLOCK, width)), 0, 1, stride=1, stride_axis=0
            )
            for g in range(per_tile)
        ]
        band = jnp.concatenate(parts, axis=0)
        band_ref[tile] = band.astype(BF16)
        band_t_ref[tile] = band.astype(BF16).T[0 : taps + BLOCK]


def notes_of(note_ref, own, span):
    window = own + span
    joined = [note_ref[b : b + 1, 0:LANES] for b in range(window)]
    same = [
        [note_ref[window + n * span + s : window + n * span + s + 1, 0:LANES] for s in range(span)]
        for n in range(own)
    ]
    reward = note_ref[window + own * span : window + own * span + 1]
    return joined, same, reward


def lane_picks(per_tile):
    lane_group = lax.broadcasted_iota(jnp.int32, (BLOCK, LANES), 1) // (LANES // per_tile)
    return [lane_group == g for g in range(per_tile)]


def shifted(x_ref, tile, b, j):
    at = SLOT * b + PRE - j
    return x_ref[tile, at : at + BLOCK, :]


def tile_lanes(tile):
    return pl.ds(pl.multiple_of(tile * LANES, LANES), LANES)


def window_of(z_ref, tile, n, same):
    span = len(same[n])
    pieces = []
    for s in range(span + 1):
        piece = z_ref[tile, BLOCK * (n + s) : BLOCK * (n + s + 1)]
        pieces.append(piece * same[n][s].astype(BF16) if s < span else piece)
    pieces.append(jnp.zeros((2 * LANES - BLOCK * (span + 1), LANES), BF16))
    return jnp.concatenate(pieces, axis=0)


def windows_of(z_ref, tile, half, same):
    return jnp.concatenate([window_of(z_ref, tile, 2 * half + i, same) for i in range(2)], axis=1)


def in_groups(count, beside, stages):
    def some(step, carry):
        now = [step * beside + side for side in range(beside)]
        kept = [None] * beside
        for stage in stages:
            kept = [stage(tile, side, got) for side, (tile, got) in enumerate(zip(now, kept))]
        return carry

    lax.fori_loop(0, count // beside, some, 0)


def blocks_of(ref, at, start, count):
    return [ref[start + BLOCK * b : start + BLOCK * (b + 1), at].astype(F32) for b in range(count)]


def fill(x_ref, tile, pieces, before, joined):
    for b, piece in enumerate(pieces):
        at = SLOT * b
        x_ref[tile, at : at + PRE] = before * joined[b]
        x_ref[tile, at + PRE : at + SLOT] = piece
        before = piece[BLOCK - PRE :]


def short(x_ref, tile, b, taps_now):
    total = taps_now[0:1] * shifted(x_ref, tile, b, 0)
    for j in range(1, taps_now.shape[0]):
        total = total + taps_now[j : j + 1] * shifted(x_ref, tile, b, j)
    return total


def key_kernel(beside, k_ref, k_near_ref, note_ref, se_ref, xk_ref, ks_ref):
    rows, channels = k_ref.shape
    own = rows // BLOCK
    later = xk_ref.shape[1] // SLOT
    span = later + 1 - own
    joined, _, _ = notes_of(note_ref, own, span)

    def filters(tile, side, _):
        at = tile_lanes(tile)
        k_taps = se_ref[1, :, at].astype(F32)
        halo = blocks_of(k_near_ref, at, rows - span * BLOCK, span)
        before = halo[0][BLOCK - PRE :]
        fill(xk_ref, tile, halo[1:] + blocks_of(k_ref, at, 0, own), before, joined[1:])
        for b in range(later):
            ks_ref[tile, BLOCK * b : BLOCK * (b + 1)] = short(xk_ref, tile, b, k_taps)

    in_groups(channels // LANES, beside, (filters,))


def forward_kernel(
    beside,
    q_ref,
    v_ref,
    up_ref,
    k_near_ref,
    near_ref,
    far_ref,
    note_ref,
    se_ref,
    band_ref,
    ks_ref,
    xq_ref,
    xk_ref,
    xv_ref,
    ks_first_ref,
    vs_ref,
    zw_ref,
    uq_ref,
    um_ref,
    z_ref,
):
    rows, channels = q_ref.shape
    own = rows // BLOCK
    window = xv_ref.shape[1] // SLOT
    span = window - own
    tiles = channels // LANES
    per_tile = band_ref.shape[1] // BLOCK
    joined, same, _ = notes_of(note_ref, own, span)
    picks = lane_picks(per_tile)

    def filters(tile, side, _):
        at = tile_lanes(tile)
        q_taps, k_taps, v_taps = (se_ref[i, :, at].astype(F32) for i in range(3))
        q_before = near_ref[rows:, at].astype(F32)[TAIL - PRE :]
        k_before, v_before = jnp.split(far_ref[:, at].astype(F32), 2)
        v_halo = blocks_of(near_ref, at, rows - span * BLOCK, span)
        fill(xv_ref, tile, v_halo + blocks_of(v_ref, at, 0, own), v_before, joined)
        fill(xk_ref, tile, blocks_of(k_near_ref, at, rows - span * BLOCK, 1), k_before, joined)
        fill(xq_ref, tile, blocks_of(q_ref, at, 0, own), q_before, joined[span:])
        for b in range(window):
            at_b = slice(BLOCK * b, BLOCK * (b + 1))
            vs = short(xv_ref, tile, b, v_taps)
            vs_ref[tile, at_b] = vs
            if b == 0:
                ks = short(xk_ref, tile, b, k_taps)
                ks_first_ref[tile] = ks
            else:
                ks = ks_ref[tile, BLOCK * (b - 1) : BLOCK * b]
            z_ref[side, at_b] = (ks * vs).astype(BF16)
        for n in range(own):
            at_n = slice(BLOCK * n, BLOCK * (n + 1))
            uq_ref[tile, at_n] = up_ref[at_n, at].astype(F32) * short(xq_ref, tile, n, q_taps)

    def medium(tile, side, _):
        at = tile_lanes(tile)
        band = band_ref[tile]
        for half in range(own // 2):
            zws = windows_of(z_ref, side, half, same)
            zw_ref[tile, half] = zws
            wide = dot(band, zws, ((1,), (0,)))
            for part in range(2):
                n = 2 * half + part
                at_n = slice(BLOCK * n, BLOCK * (n + 1))
                lanes = slice(LANES * part, LANES * (part + 1))
                m = wide[0:BLOCK, lanes]
                for g in range(1, per_tile):
                    m = jnp.where(picks[g], wide[BLOCK * g : BLOCK * (g + 1), lanes], m)
                um_ref[tile, at_n] = up_ref[at_n, at].astype(F32) * m

    in_groups(tiles, beside, (filters, medium))


def backward_kernel(
    all_channels,
    beside,
    count,
    xk_ref,
    ks_ref,
    xq_ref,
    xk_first_ref,
    xv_ref,
    ks_first_ref,
    vs_ref,
    zw_ref,
    uq_ref,
    um_ref,
    note_ref,
    band_t_ref,
    *rest,
):
    *sq_refs, out_ref, dm_ref, dz_ref, skew_ref, w_ref = rest
    tiles, rows = uq_ref.shape[0:2]
    own = rows // BLOCK
    window = xv_ref.shape[1] // SLOT
    span = window - own
    per_tile = band_t_ref.shape[2] // BLOCK
    _, same, reward = notes_of(note_ref, own, span)
    masks = [jnp.where(pick, 1.0, 0.0).astype(BF16) for pick in lane_picks(per_tile)]
    weight = reward * lax.rsqrt(summed([ref[0:1] for ref in sq_refs]) / all_channels + 1e-06)
    w_ref[...] = jnp.broadcast_to(weight, (LANES, rows)).T

    def fold(x):
        return jnp.sum(x.reshape(BLOCK // 8, 8, LANES), axis=0)

    def stack(tile, side, _):
        for n in range(own):
            at_n = slice(BLOCK * n, BLOCK * (n + 1))
            dm = (w_ref[at_n] * uq_ref[tile, at_n]).astype(BF16)
            lanes = slice(LANES * (n % 2), LANES * (n % 2 + 1))
            for g in range(per_tile):
                dm_ref[side, n // 2, BLOCK * g : BLOCK * (g + 1), lanes] = dm * masks[g]

    def middle(tile, side, _):
        band_t = band_t_ref[tile]
        pair = None
        for half in range(own // 2):
            dms = dm_ref[side, half]
            back = dot(band_t, dms, ((1,), (0,)))
            both = dot(dms, zw_ref[tile, half], ((1,), (1,)))
            pair = both if pair is None else pair + both
            for part in range(2):
                n = 2 * half + part
                lanes = slice(LANES * part, LANES * (part + 1))
                for s in range(span + 1):
                    at_s = slice(BLOCK * (n + s), BLOCK * (n + s + 1))
                    term = back[BLOCK * s : BLOCK * (s + 1), lanes]
                    if s < span:
                        term = term * same[n][s]
                    if n == 0 or s == span:
                        dz_ref[side, at_s] = term
                    else:
                        dz_ref[side, at_s] += term
        lined = pair.reshape(per_tile, BLOCK // 8, 8, 2 * LANES)
        skew = None
        for r in range(BLOCK // 8):
            rows_r = lined[:, r].reshape(per_tile * 8, 2 * LANES)
            moved = pltpu.roll(rows_r, 2 * LANES - 8 * r, 1) if r else rows_r
            skew = moved if skew is None else skew + moved
        for side_of in range(2):
            start = (side_of * tiles + tile) * per_tile * 8
            skew_ref[pl.ds(pl.multiple_of(start, 8), per_tile * 8)] = skew[
                :, LANES * side_of : LANES * (side_of + 1)
            ]

    def grads(tile, side, _):
        at = tile_lanes(tile)
        gq, gk, gv = ([jnp.zeros((8, LANES), F32) for _ in range(count)] for _ in range(3))
        for n in range(own):
            at_n = slice(BLOCK * n, BLOCK * (n + 1))
            cot_q = w_ref[at_n] * um_ref[tile, at_n]
            for j in range(count):
                gq[j] = gq[j] + fold(cot_q * shifted(xq_ref, tile, n, j))
        for b in range(window):
            at_b = slice(BLOCK * b, BLOCK * (b + 1))
            dz = dz_ref[side, at_b]
            cot_k = dz * vs_ref[tile, at_b]
            ks = ks_ref[tile, BLOCK * (b - 1) : BLOCK * b] if b else ks_first_ref[tile]
            cot_v = dz * ks
            for j in range(count):
                k_rows = shifted(xk_ref, tile, b - 1, j) if b else shifted(xk_first_ref, tile, 0, j)
                gk[j] = gk[j] + fold(cot_k * k_rows)
                gv[j] = gv[j] + fold(cot_v * shifted(xv_ref, tile, b, j))
        for i, sums in enumerate((gq, gk, gv)):
            for j in range(count):
                out_ref[8 * i + j : 8 * i + j + 1, at] = jnp.sum(sums[j], axis=0, keepdims=True)
            out_ref[8 * i + count : 8 * i + 8, at] = jnp.zeros((8 - count, LANES), F32)

    in_groups(tiles, beside, (stack, middle, grads))
    lane = lax.broadcasted_iota(jnp.int32, (2 * LANES, LANES), 0)
    tap = lax.broadcasted_iota(jnp.int32, (2 * LANES, LANES), 1)
    groups = tiles * per_tile
    totals = None
    for u in range(8):
        rows_u = jnp.concatenate(
            [skew_ref[pl.ds(8 * groups * i + u, groups, stride=8)] for i in range(2)], axis=1
        )
        high = rows_u.astype(BF16)
        low = (rows_u - high.astype(F32)).astype(BF16)
        pick = jnp.where(lane + tap == LANES + u, 1.0, 0.0).astype(BF16)
        term = dot(jnp.concatenate([high, low], axis=0), pick, ((1,), (0,)))
        totals = term if totals is None else totals + term
    totals = totals[0:groups] + totals[groups:]
    for tile in range(tiles):
        out_ref[24 : 24 + per_tile, LANES * tile : LANES * (tile + 1)] = totals[
            per_tile * tile : per_tile * (tile + 1)
        ]


def last_kernel(scale, *refs):
    *part_refs, se_ref, mr_ref = refs
    total = summed([ref[...].astype(F32) for ref in part_refs]) * scale
    tap_count = se_ref.shape[1]
    channels = total.shape[1]
    for i in range(3):
        se_ref[i] = total[8 * i : 8 * i + tap_count]
    flat = jnp.concatenate(
        [total[24:, t * LANES : (t + 1) * LANES] for t in range(channels // LANES)], axis=0
    )
    mr_ref[...] = flat


def swapped(value, axis, distance):
    count = lax.axis_size(axis)
    return lax.ppermute(value, axis, [(i, i ^ distance) for i in range(count)])


def summed_small(value, axis, beside):
    count = lax.axis_size(axis)
    if count & (count - 1):
        return [lax.psum(value, axis)], beside
    distance = 1
    while 2 * distance < count:
        got = swapped(value, axis, distance)
        if distance == 1:
            got, beside = lax.optimization_barrier((got, beside))
        value = value + got
        distance *= 2
    return [value, swapped(value, axis, distance)], beside


def spread(part, axis):
    count = lax.axis_size(axis)
    if count & (count - 1) or count < 8:
        return [lax.psum(part, axis)]
    mine = (part + swapped(part, axis, 1)).astype(BF16)
    distance = 8
    while distance < count:
        mine = (mine.astype(F32) + swapped(mine, axis, distance).astype(F32)).astype(BF16)
        distance *= 2
    return [mine] + [swapped(mine, axis, d) for d in (2, 4, 6)]


def moved_up(value, axis, steps):
    count = lax.axis_size(axis)
    return lax.ppermute(value, axis, [(i, (i + steps) % count) for i in range(count)])


def on_device(query, key, value, upstream, reward, lengths, se_filter, mr_filter):
    rows, channels = query.shape
    taps, groups = mr_filter.shape
    tap_count = se_filter.shape[1]
    tiles = channels // LANES
    per_tile = groups // tiles
    stack = per_tile * BLOCK
    own = rows // BLOCK
    span = taps // BLOCK
    window = own + span
    beside = math.gcd(tiles, 8)
    dp = lax.axis_size("dp")

    k_near = moved_up(key, "dp", 1)
    near, far, sq, notes, medium_taps, short_taps = pl.pallas_call(
        functools.partial(first_kernel, span),
        out_shape=(
            jax.ShapeDtypeStruct((rows + TAIL, channels), BF16),
            jax.ShapeDtypeStruct((2 * PRE, channels), BF16),
            jax.ShapeDtypeStruct((COPIES, rows), F32),
            jax.ShapeDtypeStruct((window + own * span + 1, rows), F32),
            jax.ShapeDtypeStruct((groups, taps), BF16),
            jax.ShapeDtypeStruct(se_filter.shape, BF16),
        ),
        in_specs=[spec(pl.ANY)] * 8,
        out_specs=(spec(),) * 6,
        scratch_shapes=[
            pltpu.VMEM((rows, channels), BF16),
            pltpu.VMEM((TAIL, channels), BF16),
            pltpu.SMEM(lengths.shape, jnp.int32),
            pltpu.VMEM((1, rows), jnp.int32),
            pltpu.SemaphoreType.DMA((8,)),
        ],
        compiler_params=pltpu.CompilerParams(vmem_limit_bytes=LIMIT),
        cost_estimate=cost(1.2),
        name="first",
    )(
        *[
            pltpu.with_memory_space_constraint(x, pltpu.HBM)
            for x in (
                lengths,
                reward.reshape(1, rows),
                query,
                key,
                value,
                upstream,
                mr_filter.T,
                se_filter,
            )
        ]
    )
    near = moved_up(near, "dp", 1)
    far = moved_up(far, "dp", 2)

    band, band_t = pl.pallas_call(
        band_kernel,
        out_shape=(
            jax.ShapeDtypeStruct((tiles, stack, 2 * LANES), BF16),
            jax.ShapeDtypeStruct((tiles, taps + BLOCK, stack), BF16),
        ),
        in_specs=[spec()],
        out_specs=(spec(),) * 2,
        scratch_shapes=[pltpu.VMEM((groups, 2 * LANES), F32)],
        compiler_params=pltpu.CompilerParams(vmem_limit_bytes=LIMIT),
        cost_estimate=cost(1.0),
        name="band",
    )(medium_taps)

    keys = pl.pallas_call(
        functools.partial(key_kernel, beside),
        out_shape=(
            jax.ShapeDtypeStruct((tiles, (window - 1) * SLOT, LANES), F32),
            jax.ShapeDtypeStruct((tiles, (window - 1) * BLOCK, LANES), F32),
        ),
        in_specs=[spec()] * 4,
        out_specs=(spec(),) * 2,
        compiler_params=pltpu.CompilerParams(vmem_limit_bytes=LIMIT),
        cost_estimate=cost(0.5),
        name="keys",
    )(key, k_near, notes, short_taps)
    squares, (band, band_t, keys) = summed_small(sq, "fsdp", (band, band_t, keys))
    kept = pl.pallas_call(
        functools.partial(forward_kernel, beside),
        out_shape=(
            jax.ShapeDtypeStruct((tiles, own * SLOT, LANES), F32),
            jax.ShapeDtypeStruct((tiles, SLOT, LANES), F32),
            jax.ShapeDtypeStruct((tiles, window * SLOT, LANES), F32),
            jax.ShapeDtypeStruct((tiles, BLOCK, LANES), F32),
            jax.ShapeDtypeStruct((tiles, window * BLOCK, LANES), F32),
            jax.ShapeDtypeStruct((tiles, own // 2, 2 * LANES, 2 * LANES), BF16),
            jax.ShapeDtypeStruct((tiles, rows, LANES), F32),
            jax.ShapeDtypeStruct((tiles, rows, LANES), F32),
        ),
        in_specs=[spec()] * 10,
        out_specs=(spec(),) * 8,
        scratch_shapes=[pltpu.VMEM((beside, window * BLOCK, LANES), BF16)],
        compiler_params=pltpu.CompilerParams(vmem_limit_bytes=LIMIT),
        cost_estimate=cost(2.0),
        name="forward",
    )(query, value, upstream, k_near, near, far, notes, short_taps, band, keys[1])
    part = pl.pallas_call(
        functools.partial(
            backward_kernel, float(channels * lax.axis_size("fsdp")), beside, tap_count
        ),
        out_shape=jax.ShapeDtypeStruct((24 + per_tile, channels), F32),
        in_specs=[spec()] * (12 + len(squares)),
        out_specs=spec(),
        scratch_shapes=[
            pltpu.VMEM((beside, own // 2, stack, 2 * LANES), BF16),
            pltpu.VMEM((beside, window * BLOCK, LANES), F32),
            pltpu.VMEM((2 * groups * 8, LANES), F32),
            pltpu.VMEM((rows, LANES), F32),
        ],
        compiler_params=pltpu.CompilerParams(vmem_limit_bytes=LIMIT),
        name="backward",
    )(*keys, *kept, notes, band_t, *squares)

    parts = spread(part, "dp")
    grad_se, grad_mr = pl.pallas_call(
        functools.partial(last_kernel, 1.0 / rows),
        out_shape=(
            jax.ShapeDtypeStruct((3, tap_count, channels), F32),
            jax.ShapeDtypeStruct((groups, taps), F32),
        ),
        in_specs=[spec()] * len(parts),
        out_specs=(spec(),) * 2,
        compiler_params=pltpu.CompilerParams(vmem_limit_bytes=LIMIT),
        name="last",
    )(*parts)
    return grad_se, grad_mr.T


def solution(mesh):
    in_specs = (
        P("dp", "fsdp"),
        P("dp", "fsdp"),
        P("dp", "fsdp"),
        P("dp", "fsdp"),
        P("dp"),
        P(),
        P(None, None, "fsdp"),
        P(None, "fsdp"),
    )
    out_specs = (P(None, None, "fsdp"), P(None, "fsdp"))
    return jax.shard_map(
        on_device, mesh=mesh, in_specs=in_specs, out_specs=out_specs, check_vma=False
    )
```

```python
import functools
import math

import jax
import jax.numpy as jnp
from jax import lax
from jax.experimental import pallas as pl
from jax.experimental.pallas import tpu as pltpu
from jax.sharding import PartitionSpec as P

BLOCK = 32
LANES = 128
TAIL = 16
PRE = 8
SLOT = PRE + BLOCK
LIMIT = 24 * 1024 * 1024
COPIES = 64
F32 = jnp.float32
BF16 = jnp.bfloat16


def spec(space=pltpu.VMEM):
    return pl.BlockSpec(memory_space=space)


def cost(micros):
    return pl.CostEstimate(flops=1, bytes_accessed=int(micros * 3.6e6), transcendentals=0)


def summed(parts):
    while len(parts) > 1:
        parts = [sum(parts[i + 1 : i + 2], parts[i]) for i in range(0, len(parts), 2)]
    return parts[0]


def dot(a, b, contract, precision=None):
    return lax.dot_general(
        a, b, ((contract[0], contract[1]), ((), ())), precision=precision, preferred_element_type=F32
    )


def doc_of(lengths_ref, block):
    count = jnp.int32(0)
    end = jnp.int32(0)
    for i in range(lengths_ref.shape[0]):
        end = end + lengths_ref[i]
        count = count + jnp.where(block >= end, 1, 0)
    return jnp.where(block >= 0, count, -1)


def first_kernel(
    span,
    lengths_ref,
    reward_ref,
    q_ref,
    k_ref,
    v_ref,
    up_ref,
    h_ref,
    se_ref,
    near_ref,
    far_ref,
    sq_ref,
    note_ref,
    h_out_ref,
    se_out_ref,
    up_here,
    k_here,
    lengths_here,
    reward_here,
    sems,
):
    rows, channels = k_ref.shape
    tail = pl.ds(rows - TAIL, TAIL)
    pieces = (
        (up_ref, up_here),
        (v_ref, near_ref.at[pl.ds(0, rows)]),
        (q_ref.at[tail], near_ref.at[pl.ds(rows, TAIL)]),
        (k_ref.at[tail], k_here),
        (lengths_ref, lengths_here),
        (reward_ref, reward_here),
        (h_ref, h_out_ref),
        (se_ref, se_out_ref),
    )
    copies = [
        pltpu.make_async_copy(source, target, sems.at[i]) for i, (source, target) in enumerate(pieces)
    ]
    for copy in copies:
        copy.start()
    copies[4].wait()
    copies[5].wait()
    own = rows // BLOCK
    window = span + own
    first = lax.axis_index("dp") * own
    docs = [doc_of(lengths_here, first + b) for b in range(-span - 1, own)]
    notes = [(docs[b + 1] == docs[b]) & (docs[b] >= 0) for b in range(window)]
    docs = docs[1:]
    notes = notes + [docs[n + s] == docs[n + span] for n in range(own) for s in range(span)]
    for i, note in enumerate(notes):
        note_ref[i : i + 1] = jnp.full((1, rows), jnp.where(note, 1.0, 0.0).astype(F32))
    note_ref[len(notes) : len(notes) + 1] = reward_here[...].astype(F32) * 0.25
    copies[0].wait()
    total = jnp.zeros((rows, LANES), F32)
    for tile in range(channels // LANES):
        part = up_here[:, tile * LANES : (tile + 1) * LANES].astype(F32)
        total = total + part * part
    sq_ref[...] = jnp.broadcast_to(jnp.sum(total.T, axis=0, keepdims=True), sq_ref.shape)
    for copy in copies[1:4] + copies[6:]:
        copy.wait()
    tails = [ref[...].astype(F32)[TAIL - PRE :] for ref in (k_here, near_ref.at[tail])]
    far_ref[...] = jnp.concatenate(tails, axis=0).astype(BF16)


def band_kernel(h_ref, band_ref, band_t_ref, row_ref):
    groups, taps = h_ref.shape
    tiles = band_ref.shape[0]
    per_tile = groups // tiles
    width = band_ref.shape[2]
    tap = lax.broadcasted_iota(jnp.int32, (taps, width), 0)
    lane = lax.broadcasted_iota(jnp.int32, (taps, width), 1)
    flip = jnp.where(tap + lane == taps, 1.0, 0.0).astype(F32)
    row_ref[...] = dot(h_ref[...], flip.astype(BF16), ((1,), (0,)))

    for tile in range(tiles):
        rows = row_ref[tile * per_tile : (tile + 1) * per_tile]
        parts = [
            pltpu.roll(
                jnp.broadcast_to(rows[g : g + 1], (BLOCK, width)), 0, 1, stride=1, stride_axis=0
            )
            for g in range(per_tile)
        ]
        band = jnp.concatenate(parts, axis=0)
        band_ref[tile] = band.astype(BF16)
        band_t_ref[tile] = band.astype(BF16).T[0 : taps + BLOCK]


def notes_of(note_ref, own, span):
    window = own + span
    joined = [note_ref[b : b + 1, 0:LANES] for b in range(window)]
    same = [
        [note_ref[window + n * span + s : window + n * span + s + 1, 0:LANES] for s in range(span)]
        for n in range(own)
    ]
    reward = note_ref[window + own * span : window + own * span + 1]
    return joined, same, reward


def lane_picks(per_tile):
    lane_group = lax.broadcasted_iota(jnp.int32, (BLOCK, LANES), 1) // (LANES // per_tile)
    return [lane_group == g for g in range(per_tile)]


def shifted(x_ref, tile, b, j):
    at = SLOT * b + PRE - j
    return x_ref[tile, at : at + BLOCK, :]


def tile_lanes(tile):
    return pl.ds(pl.multiple_of(tile * LANES, LANES), LANES)


def window_of(z_ref, tile, n, same):
    span = len(same[n])
    pieces = []
    for s in range(span + 1):
        piece = z_ref[tile, BLOCK * (n + s) : BLOCK * (n + s + 1)]
        pieces.append(piece * same[n][s].astype(BF16) if s < span else piece)
    pieces.append(jnp.zeros((2 * LANES - BLOCK * (span + 1), LANES), BF16))
    return jnp.concatenate(pieces, axis=0)


def windows_of(z_ref, tile, half, same):
    return jnp.concatenate([window_of(z_ref, tile, 2 * half + i, same) for i in range(2)], axis=1)


def in_groups(count, beside, stages):
    def some(step, carry):
        now = [step * beside + side for side in range(beside)]
        kept = [None] * beside
        for stage in stages:
            kept = [stage(tile, side, got) for side, (tile, got) in enumerate(zip(now, kept))]
        return carry

    lax.fori_loop(0, count // beside, some, 0)


def blocks_of(ref, at, start, count):
    return [ref[start + BLOCK * b : start + BLOCK * (b + 1), at].astype(F32) for b in range(count)]


def fill(x_ref, tile, pieces, before, joined):
    for b, piece in enumerate(pieces):
        at = SLOT * b
        x_ref[tile, at : at + PRE] = before * joined[b]
        x_ref[tile, at + PRE : at + SLOT] = piece
        before = piece[BLOCK - PRE :]


def short(x_ref, tile, b, taps_now):
    total = taps_now[0:1] * shifted(x_ref, tile, b, 0)
    for j in range(1, taps_now.shape[0]):
        total = total + taps_now[j : j + 1] * shifted(x_ref, tile, b, j)
    return total


def key_kernel(beside, k_ref, k_near_ref, note_ref, se_ref, xk_ref, ks_ref):
    rows, channels = k_ref.shape
    own = rows // BLOCK
    later = xk_ref.shape[1] // SLOT
    span = later + 1 - own
    joined, _, _ = notes_of(note_ref, own, span)

    def filters(tile, side, _):
        at = tile_lanes(tile)
        k_taps = se_ref[1, :, at].astype(F32)
        halo = blocks_of(k_near_ref, at, rows - span * BLOCK, span)
        before = halo[0][BLOCK - PRE :]
        fill(xk_ref, tile, halo[1:] + blocks_of(k_ref, at, 0, own), before, joined[1:])
        for b in range(later):
            ks_ref[tile, BLOCK * b : BLOCK * (b + 1)] = short(xk_ref, tile, b, k_taps)

    in_groups(channels // LANES, beside, (filters,))


def forward_kernel(
    beside,
    q_ref,
    v_ref,
    up_ref,
    k_near_ref,
    near_ref,
    far_ref,
    note_ref,
    se_ref,
    band_ref,
    ks_ref,
    xq_ref,
    xk_ref,
    xv_ref,
    ks_first_ref,
    vs_ref,
    zw_ref,
    uq_ref,
    um_ref,
    z_ref,
):
    rows, channels = q_ref.shape
    own = rows // BLOCK
    window = xv_ref.shape[1] // SLOT
    span = window - own
    tiles = channels // LANES
    per_tile = band_ref.shape[1] // BLOCK
    joined, same, _ = notes_of(note_ref, own, span)
    picks = lane_picks(per_tile)

    def filters(tile, side, _):
        at = tile_lanes(tile)
        q_taps, k_taps, v_taps = (se_ref[i, :, at].astype(F32) for i in range(3))
        q_before = near_ref[rows:, at].astype(F32)[TAIL - PRE :]
        k_before, v_before = jnp.split(far_ref[:, at].astype(F32), 2)
        v_halo = blocks_of(near_ref, at, rows - span * BLOCK, span)
        fill(xv_ref, tile, v_halo + blocks_of(v_ref, at, 0, own), v_before, joined)
        fill(xk_ref, tile, blocks_of(k_near_ref, at, rows - span * BLOCK, 1), k_before, joined)
        fill(xq_ref, tile, blocks_of(q_ref, at, 0, own), q_before, joined[span:])
        for b in range(window):
            at_b = slice(BLOCK * b, BLOCK * (b + 1))
            vs = short(xv_ref, tile, b, v_taps)
            vs_ref[tile, at_b] = vs
            if b == 0:
                ks = short(xk_ref, tile, b, k_taps)
                ks_first_ref[tile] = ks
            else:
                ks = ks_ref[tile, BLOCK * (b - 1) : BLOCK * b]
            z_ref[side, at_b] = (ks * vs).astype(BF16)
        for n in range(own):
            at_n = slice(BLOCK * n, BLOCK * (n + 1))
            uq_ref[tile, at_n] = up_ref[at_n, at].astype(F32) * short(xq_ref, tile, n, q_taps)

    def medium(tile, side, _):
        at = tile_lanes(tile)
        band = band_ref[tile]
        for half in range(own // 2):
            zws = windows_of(z_ref, side, half, same)
            zw_ref[tile, half] = zws
            wide = dot(band, zws, ((1,), (0,)))
            for part in range(2):
                n = 2 * half + part
                at_n = slice(BLOCK * n, BLOCK * (n + 1))
                lanes = slice(LANES * part, LANES * (part + 1))
                m = wide[0:BLOCK, lanes]
                for g in range(1, per_tile):
                    m = jnp.where(picks[g], wide[BLOCK * g : BLOCK * (g + 1), lanes], m)
                um_ref[tile, at_n] = up_ref[at_n, at].astype(F32) * m

    in_groups(tiles, beside, (filters, medium))


def backward_kernel(
    all_channels,
    beside,
    count,
    xk_ref,
    ks_ref,
    xq_ref,
    xk_first_ref,
    xv_ref,
    ks_first_ref,
    vs_ref,
    zw_ref,
    uq_ref,
    um_ref,
    note_ref,
    band_t_ref,
    *rest,
):
    *sq_refs, out_ref, dm_ref, dz_ref, skew_ref, w_ref = rest
    tiles, rows = uq_ref.shape[0:2]
    own = rows // BLOCK
    window = xv_ref.shape[1] // SLOT
    span = window - own
    per_tile = band_t_ref.shape[2] // BLOCK
    _, same, reward = notes_of(note_ref, own, span)
    masks = [jnp.where(pick, 1.0, 0.0).astype(BF16) for pick in lane_picks(per_tile)]
    weight = reward * lax.rsqrt(summed([ref[0:1] for ref in sq_refs]) / all_channels + 1e-06)
    w_ref[...] = jnp.broadcast_to(weight, (LANES, rows)).T

    def fold(x):
        return jnp.sum(x.reshape(BLOCK // 8, 8, LANES), axis=0)

    def stack(tile, side, _):
        for n in range(own):
            at_n = slice(BLOCK * n, BLOCK * (n + 1))
            dm = (w_ref[at_n] * uq_ref[tile, at_n]).astype(BF16)
            lanes = slice(LANES * (n % 2), LANES * (n % 2 + 1))
            for g in range(per_tile):
                dm_ref[side, n // 2, BLOCK * g : BLOCK * (g + 1), lanes] = dm * masks[g]

    def middle(tile, side, _):
        band_t = band_t_ref[tile]
        pair = None
        for half in range(own // 2):
            dms = dm_ref[side, half]
            back = dot(band_t, dms, ((1,), (0,)))
            both = dot(dms, zw_ref[tile, half], ((1,), (1,)))
            pair = both if pair is None else pair + both
            for part in range(2):
                n = 2 * half + part
                lanes = slice(LANES * part, LANES * (part + 1))
                for s in range(span + 1):
                    at_s = slice(BLOCK * (n + s), BLOCK * (n + s + 1))
                    term = back[BLOCK * s : BLOCK * (s + 1), lanes]
                    if s < span:
                        term = term * same[n][s]
                    if n == 0 or s == span:
                        dz_ref[side, at_s] = term
                    else:
                        dz_ref[side, at_s] += term
        lined = pair.reshape(per_tile, BLOCK // 8, 8, 2 * LANES)
        skew = None
        for r in range(BLOCK // 8):
            rows_r = lined[:, r].reshape(per_tile * 8, 2 * LANES)
            moved = pltpu.roll(rows_r, 2 * LANES - 8 * r, 1) if r else rows_r
            skew = moved if skew is None else skew + moved
        for side_of in range(2):
            start = (side_of * tiles + tile) * per_tile * 8
            skew_ref[pl.ds(pl.multiple_of(start, 8), per_tile * 8)] = skew[
                :, LANES * side_of : LANES * (side_of + 1)
            ]

    def grads(tile, side, _):
        at = tile_lanes(tile)
        gq, gk, gv = ([jnp.zeros((8, LANES), F32) for _ in range(count)] for _ in range(3))
        for n in range(own):
            at_n = slice(BLOCK * n, BLOCK * (n + 1))
            cot_q = w_ref[at_n] * um_ref[tile, at_n]
            for j in range(count):
                gq[j] = gq[j] + fold(cot_q * shifted(xq_ref, tile, n, j))
        for b in range(window):
            at_b = slice(BLOCK * b, BLOCK * (b + 1))
            dz = dz_ref[side, at_b]
            cot_k = dz * vs_ref[tile, at_b]
            ks = ks_ref[tile, BLOCK * (b - 1) : BLOCK * b] if b else ks_first_ref[tile]
            cot_v = dz * ks
            for j in range(count):
                k_rows = shifted(xk_ref, tile, b - 1, j) if b else shifted(xk_first_ref, tile, 0, j)
                gk[j] = gk[j] + fold(cot_k * k_rows)
                gv[j] = gv[j] + fold(cot_v * shifted(xv_ref, tile, b, j))
        for i, sums in enumerate((gq, gk, gv)):
            for j in range(count):
                out_ref[8 * i + j : 8 * i + j + 1, at] = jnp.sum(sums[j], axis=0, keepdims=True)
            out_ref[8 * i + count : 8 * i + 8, at] = jnp.zeros((8 - count, LANES), F32)

    in_groups(tiles, beside, (stack, middle, grads))
    lane = lax.broadcasted_iota(jnp.int32, (2 * LANES, LANES), 0)
    tap = lax.broadcasted_iota(jnp.int32, (2 * LANES, LANES), 1)
    groups = tiles * per_tile
    totals = None
    for u in range(8):
        rows_u = jnp.concatenate(
            [skew_ref[pl.ds(8 * groups * i + u, groups, stride=8)] for i in range(2)], axis=1
        )
        high = rows_u.astype(BF16)
        low = (rows_u - high.astype(F32)).astype(BF16)
        pick = jnp.where(lane + tap == LANES + u, 1.0, 0.0).astype(BF16)
        term = dot(jnp.concatenate([high, low], axis=0), pick, ((1,), (0,)))
        totals = term if totals is None else totals + term
    totals = totals[0:groups] + totals[groups:]
    for tile in range(tiles):
        out_ref[24 : 24 + per_tile, LANES * tile : LANES * (tile + 1)] = totals[
            per_tile * tile : per_tile * (tile + 1)
        ]


def last_kernel(scale, *refs):
    *part_refs, se_ref, mr_ref = refs
    total = summed([ref[...].astype(F32) for ref in part_refs]) * scale
    tap_count = se_ref.shape[1]
    channels = total.shape[1]
    for i in range(3):
        se_ref[i] = total[8 * i : 8 * i + tap_count]
    flat = jnp.concatenate(
        [total[24:, t * LANES : (t + 1) * LANES] for t in range(channels // LANES)], axis=0
    )
    mr_ref[...] = flat


def swapped(value, axis, distance):
    count = lax.axis_size(axis)
    return lax.ppermute(value, axis, [(i, i ^ distance) for i in range(count)])


def summed_small(value, axis, beside):
    count = lax.axis_size(axis)
    if count & (count - 1):
        return [lax.psum(value, axis)], beside
    distance = 1
    while 2 * distance < count:
        got = swapped(value, axis, distance)
        if distance == 1:
            got, beside = lax.optimization_barrier((got, beside))
        value = value + got
        distance *= 2
    return [value, swapped(value, axis, distance)], beside


def spread(part, axis):
    count = lax.axis_size(axis)
    if count & (count - 1) or count < 8:
        return [lax.psum(part, axis)]
    mine = (part + swapped(part, axis, 1)).astype(BF16)
    distance = 8
    while distance < count:
        mine = (mine.astype(F32) + swapped(mine, axis, distance).astype(F32)).astype(BF16)
        distance *= 2
    return [mine] + [swapped(mine, axis, d) for d in (2, 4, 6)]


def moved_up(value, axis, steps):
    count = lax.axis_size(axis)
    return lax.ppermute(value, axis, [(i, (i + steps) % count) for i in range(count)])


def on_device(query, key, value, upstream, reward, lengths, se_filter, mr_filter):
    rows, channels = query.shape
    taps, groups = mr_filter.shape
    tap_count = se_filter.shape[1]
    tiles = channels // LANES
    per_tile = groups // tiles
    stack = per_tile * BLOCK
    own = rows // BLOCK
    span = taps // BLOCK
    window = own + span
    beside = math.gcd(tiles, 8)
    dp = lax.axis_size("dp")

    k_near = moved_up(key, "dp", 1)
    near, far, sq, notes, medium_taps, short_taps = pl.pallas_call(
        functools.partial(first_kernel, span),
        out_shape=(
            jax.ShapeDtypeStruct((rows + TAIL, channels), BF16),
            jax.ShapeDtypeStruct((2 * PRE, channels), BF16),
            jax.ShapeDtypeStruct((COPIES, rows), F32),
            jax.ShapeDtypeStruct((window + own * span + 1, rows), F32),
            jax.ShapeDtypeStruct((groups, taps), BF16),
            jax.ShapeDtypeStruct(se_filter.shape, BF16),
        ),
        in_specs=[spec(pl.ANY)] * 8,
        out_specs=(spec(),) * 6,
        scratch_shapes=[
            pltpu.VMEM((rows, channels), BF16),
            pltpu.VMEM((TAIL, channels), BF16),
            pltpu.SMEM(lengths.shape, jnp.int32),
            pltpu.VMEM((1, rows), jnp.int32),
            pltpu.SemaphoreType.DMA((8,)),
        ],
        compiler_params=pltpu.CompilerParams(vmem_limit_bytes=LIMIT),
        cost_estimate=cost(1.2),
        name="first",
    )(
        *[
            pltpu.with_memory_space_constraint(x, pltpu.HBM)
            for x in (
                lengths,
                reward.reshape(1, rows),
                query,
                key,
                value,
                upstream,
                mr_filter.T,
                se_filter,
            )
        ]
    )
    near = moved_up(near, "dp", 1)
    far = moved_up(far, "dp", 2)

    band, band_t = pl.pallas_call(
        band_kernel,
        out_shape=(
            jax.ShapeDtypeStruct((tiles, stack, 2 * LANES), BF16),
            jax.ShapeDtypeStruct((tiles, taps + BLOCK, stack), BF16),
        ),
        in_specs=[spec()],
        out_specs=(spec(),) * 2,
        scratch_shapes=[pltpu.VMEM((groups, 2 * LANES), F32)],
        compiler_params=pltpu.CompilerParams(vmem_limit_bytes=LIMIT),
        cost_estimate=cost(1.0),
        name="band",
    )(medium_taps)

    squares, (band, band_t, k_near) = summed_small(sq, "fsdp", (band, band_t, k_near))
    keys = pl.pallas_call(
        functools.partial(key_kernel, beside),
        out_shape=(
            jax.ShapeDtypeStruct((tiles, (window - 1) * SLOT, LANES), F32),
            jax.ShapeDtypeStruct((tiles, (window - 1) * BLOCK, LANES), F32),
        ),
        in_specs=[spec()] * 4,
        out_specs=(spec(),) * 2,
        compiler_params=pltpu.CompilerParams(vmem_limit_bytes=LIMIT),
        cost_estimate=cost(0.5),
        name="keys",
    )(key, k_near, notes, short_taps)
    kept = pl.pallas_call(
        functools.partial(forward_kernel, beside),
        out_shape=(
            jax.ShapeDtypeStruct((tiles, own * SLOT, LANES), F32),
            jax.ShapeDtypeStruct((tiles, SLOT, LANES), F32),
            jax.ShapeDtypeStruct((tiles, window * SLOT, LANES), F32),
            jax.ShapeDtypeStruct((tiles, BLOCK, LANES), F32),
            jax.ShapeDtypeStruct((tiles, window * BLOCK, LANES), F32),
            jax.ShapeDtypeStruct((tiles, own // 2, 2 * LANES, 2 * LANES), BF16),
            jax.ShapeDtypeStruct((tiles, rows, LANES), F32),
            jax.ShapeDtypeStruct((tiles, rows, LANES), F32),
        ),
        in_specs=[spec()] * 10,
        out_specs=(spec(),) * 8,
        scratch_shapes=[pltpu.VMEM((beside, window * BLOCK, LANES), BF16)],
        compiler_params=pltpu.CompilerParams(vmem_limit_bytes=LIMIT),
        cost_estimate=cost(2.0),
        name="forward",
    )(query, value, upstream, k_near, near, far, notes, short_taps, band, keys[1])
    part = pl.pallas_call(
        functools.partial(
            backward_kernel, float(channels * lax.axis_size("fsdp")), beside, tap_count
        ),
        out_shape=jax.ShapeDtypeStruct((24 + per_tile, channels), F32),
        in_specs=[spec()] * (12 + len(squares)),
        out_specs=spec(),
        scratch_shapes=[
            pltpu.VMEM((beside, own // 2, stack, 2 * LANES), BF16),
            pltpu.VMEM((beside, window * BLOCK, LANES), F32),
            pltpu.VMEM((2 * groups * 8 + 8, LANES), F32),
            pltpu.VMEM((rows, LANES), F32),
        ],
        compiler_params=pltpu.CompilerParams(vmem_limit_bytes=LIMIT),
        name="backward",
    )(*keys, *kept, notes, band_t, *squares)

    parts = spread(part, "dp")
    grad_se, grad_mr = pl.pallas_call(
        functools.partial(last_kernel, 1.0 / rows),
        out_shape=(
            jax.ShapeDtypeStruct((3, tap_count, channels), F32),
            jax.ShapeDtypeStruct((groups, taps), F32),
        ),
        in_specs=[spec()] * len(parts),
        out_specs=(spec(),) * 2,
        compiler_params=pltpu.CompilerParams(vmem_limit_bytes=LIMIT),
        name="last",
    )(*parts)
    return grad_se, grad_mr.T


def solution(mesh):
    in_specs = (
        P("dp", "fsdp"),
        P("dp", "fsdp"),
        P("dp", "fsdp"),
        P("dp", "fsdp"),
        P("dp"),
        P(),
        P(None, None, "fsdp"),
        P(None, "fsdp"),
    )
    out_specs = (P(None, None, "fsdp"), P(None, "fsdp"))
    return jax.shard_map(
        on_device, mesh=mesh, in_specs=in_specs, out_specs=out_specs, check_vma=False
    )
```

```python
import functools
import math

import jax
import jax.numpy as jnp
from jax import lax
from jax.experimental import pallas as pl
from jax.experimental.pallas import tpu as pltpu
from jax.sharding import PartitionSpec as P

BLOCK = 32
LANES = 128
TAIL = 16
PRE = 8
SLOT = PRE + BLOCK
LIMIT = 24 * 1024 * 1024
COPIES = 64
F32 = jnp.float32
BF16 = jnp.bfloat16


def spec(space=pltpu.VMEM):
    return pl.BlockSpec(memory_space=space)


def cost(micros):
    return pl.CostEstimate(flops=1, bytes_accessed=int(micros * 3.6e6), transcendentals=0)


def summed(parts):
    while len(parts) > 1:
        parts = [sum(parts[i + 1 : i + 2], parts[i]) for i in range(0, len(parts), 2)]
    return parts[0]


def dot(a, b, contract, precision=None):
    return lax.dot_general(
        a, b, ((contract[0], contract[1]), ((), ())), precision=precision, preferred_element_type=F32
    )


def doc_of(lengths_ref, block):
    count = jnp.int32(0)
    end = jnp.int32(0)
    for i in range(lengths_ref.shape[0]):
        end = end + lengths_ref[i]
        count = count + jnp.where(block >= end, 1, 0)
    return jnp.where(block >= 0, count, -1)


def first_kernel(
    span,
    lengths_ref,
    reward_ref,
    q_ref,
    k_ref,
    v_ref,
    up_ref,
    h_ref,
    se_ref,
    near_ref,
    far_ref,
    sq_ref,
    note_ref,
    h_out_ref,
    se_out_ref,
    up_here,
    k_here,
    lengths_here,
    reward_here,
    sems,
):
    rows, channels = k_ref.shape
    tail = pl.ds(rows - TAIL, TAIL)
    pieces = (
        (up_ref, up_here),
        (v_ref, near_ref.at[pl.ds(0, rows)]),
        (q_ref.at[tail], near_ref.at[pl.ds(rows, TAIL)]),
        (k_ref.at[tail], k_here),
        (lengths_ref, lengths_here),
        (reward_ref, reward_here),
        (h_ref, h_out_ref),
        (se_ref, se_out_ref),
    )
    copies = [
        pltpu.make_async_copy(source, target, sems.at[i]) for i, (source, target) in enumerate(pieces)
    ]
    for copy in copies:
        copy.start()
    copies[4].wait()
    copies[5].wait()
    own = rows // BLOCK
    window = span + own
    first = lax.axis_index("dp") * own
    docs = [doc_of(lengths_here, first + b) for b in range(-span - 1, own)]
    notes = [(docs[b + 1] == docs[b]) & (docs[b] >= 0) for b in range(window)]
    docs = docs[1:]
    notes = notes + [docs[n + s] == docs[n + span] for n in range(own) for s in range(span)]
    for i, note in enumerate(notes):
        note_ref[i : i + 1] = jnp.full((1, rows), jnp.where(note, 1.0, 0.0).astype(F32))
    note_ref[len(notes) : len(notes) + 1] = reward_here[...].astype(F32) * 0.25
    copies[0].wait()
    total = jnp.zeros((rows, LANES), F32)
    for tile in range(channels // LANES):
        part = up_here[:, tile * LANES : (tile + 1) * LANES].astype(F32)
        total = total + part * part
    sq_ref[...] = jnp.broadcast_to(jnp.sum(total.T, axis=0, keepdims=True), sq_ref.shape)
    for copy in copies[1:4] + copies[6:]:
        copy.wait()
    tails = [ref[...].astype(F32)[TAIL - PRE :] for ref in (k_here, near_ref.at[tail])]
    far_ref[...] = jnp.concatenate(tails, axis=0).astype(BF16)


def band_kernel(h_ref, band_ref, band_t_ref, row_ref):
    groups, taps = h_ref.shape
    tiles = band_ref.shape[0]
    per_tile = groups // tiles
    width = band_ref.shape[2]
    tap = lax.broadcasted_iota(jnp.int32, (taps, width), 0)
    lane = lax.broadcasted_iota(jnp.int32, (taps, width), 1)
    flip = jnp.where(tap + lane == taps, 1.0, 0.0).astype(F32)
    row_ref[...] = dot(h_ref[...], flip.astype(BF16), ((1,), (0,)))

    for tile in range(tiles):
        rows = row_ref[tile * per_tile : (tile + 1) * per_tile]
        parts = [
            pltpu.roll(
                jnp.broadcast_to(rows[g : g + 1], (BLOCK, width)), 0, 1, stride=1, stride_axis=0
            )
            for g in range(per_tile)
        ]
        band = jnp.concatenate(parts, axis=0)
        band_ref[tile] = band.astype(BF16)
        band_t_ref[tile] = band.astype(BF16).T[0 : taps + BLOCK]


def notes_of(note_ref, own, span):
    window = own + span
    joined = [note_ref[b : b + 1, 0:LANES] for b in range(window)]
    same = [
        [note_ref[window + n * span + s : window + n * span + s + 1, 0:LANES] for s in range(span)]
        for n in range(own)
    ]
    reward = note_ref[window + own * span : window + own * span + 1]
    return joined, same, reward


def lane_picks(per_tile):
    lane_group = lax.broadcasted_iota(jnp.int32, (BLOCK, LANES), 1) // (LANES // per_tile)
    return [lane_group == g for g in range(per_tile)]


def shifted(x_ref, tile, b, j):
    at = SLOT * b + PRE - j
    return x_ref[tile, at : at + BLOCK, :]


def tile_lanes(tile):
    return pl.ds(pl.multiple_of(tile * LANES, LANES), LANES)


def window_of(z_ref, tile, n, same):
    span = len(same[n])
    pieces = []
    for s in range(span + 1):
        piece = z_ref[tile, BLOCK * (n + s) : BLOCK * (n + s + 1)]
        pieces.append(piece * same[n][s].astype(BF16) if s < span else piece)
    pieces.append(jnp.zeros((2 * LANES - BLOCK * (span + 1), LANES), BF16))
    return jnp.concatenate(pieces, axis=0)


def windows_of(z_ref, tile, half, same):
    return jnp.concatenate([window_of(z_ref, tile, 2 * half + i, same) for i in range(2)], axis=1)


def in_groups(count, beside, stages):
    def some(step, carry):
        now = [step * beside + side for side in range(beside)]
        kept = [None] * beside
        for stage in stages:
            kept = [stage(tile, side, got) for side, (tile, got) in enumerate(zip(now, kept))]
        return carry

    lax.fori_loop(0, count // beside, some, 0)


def blocks_of(ref, at, start, count):
    return [ref[start + BLOCK * b : start + BLOCK * (b + 1), at].astype(F32) for b in range(count)]


def fill(x_ref, tile, pieces, before, joined):
    for b, piece in enumerate(pieces):
        at = SLOT * b
        x_ref[tile, at : at + PRE] = before * joined[b]
        x_ref[tile, at + PRE : at + SLOT] = piece
        before = piece[BLOCK - PRE :]


def short(x_ref, tile, b, taps_now):
    total = taps_now[0:1] * shifted(x_ref, tile, b, 0)
    for j in range(1, taps_now.shape[0]):
        total = total + taps_now[j : j + 1] * shifted(x_ref, tile, b, j)
    return total


def key_kernel(beside, k_ref, k_near_ref, note_ref, se_ref, xk_ref, ks_ref):
    rows, channels = k_ref.shape
    own = rows // BLOCK
    later = xk_ref.shape[1] // SLOT
    span = later + 1 - own
    joined, _, _ = notes_of(note_ref, own, span)

    def filters(tile, side, _):
        at = tile_lanes(tile)
        k_taps = se_ref[1, :, at].astype(F32)
        halo = blocks_of(k_near_ref, at, rows - span * BLOCK, span)
        before = halo[0][BLOCK - PRE :]
        fill(xk_ref, tile, halo[1:] + blocks_of(k_ref, at, 0, own), before, joined[1:])
        for b in range(later):
            ks_ref[tile, BLOCK * b : BLOCK * (b + 1)] = short(xk_ref, tile, b, k_taps)

    in_groups(channels // LANES, beside, (filters,))


def forward_kernel(
    beside,
    q_ref,
    v_ref,
    up_ref,
    k_near_ref,
    near_ref,
    far_ref,
    note_ref,
    se_ref,
    band_ref,
    ks_ref,
    xq_ref,
    xk_ref,
    xv_ref,
    ks_first_ref,
    vs_ref,
    zw_ref,
    uq_ref,
    um_ref,
    z_ref,
):
    rows, channels = q_ref.shape
    own = rows // BLOCK
    window = xv_ref.shape[1] // SLOT
    span = window - own
    tiles = channels // LANES
    per_tile = band_ref.shape[1] // BLOCK
    joined, same, _ = notes_of(note_ref, own, span)
    picks = lane_picks(per_tile)

    def filters(tile, side, _):
        at = tile_lanes(tile)
        q_taps, k_taps, v_taps = (se_ref[i, :, at].astype(F32) for i in range(3))
        q_before = near_ref[rows:, at].astype(F32)[TAIL - PRE :]
        k_before, v_before = jnp.split(far_ref[:, at].astype(F32), 2)
        v_halo = blocks_of(near_ref, at, rows - span * BLOCK, span)
        fill(xv_ref, tile, v_halo + blocks_of(v_ref, at, 0, own), v_before, joined)
        fill(xk_ref, tile, blocks_of(k_near_ref, at, rows - span * BLOCK, 1), k_before, joined)
        fill(xq_ref, tile, blocks_of(q_ref, at, 0, own), q_before, joined[span:])
        for b in range(window):
            at_b = slice(BLOCK * b, BLOCK * (b + 1))
            vs = short(xv_ref, tile, b, v_taps)
            vs_ref[tile, at_b] = vs
            if b == 0:
                ks = short(xk_ref, tile, b, k_taps)
                ks_first_ref[tile] = ks
            else:
                ks = ks_ref[tile, BLOCK * (b - 1) : BLOCK * b]
            z_ref[side, at_b] = (ks * vs).astype(BF16)
        for n in range(own):
            at_n = slice(BLOCK * n, BLOCK * (n + 1))
            uq_ref[tile, at_n] = up_ref[at_n, at].astype(F32) * short(xq_ref, tile, n, q_taps)

    def medium(tile, side, _):
        at = tile_lanes(tile)
        band = band_ref[tile]
        for half in range(own // 2):
            zws = windows_of(z_ref, side, half, same)
            zw_ref[tile, half] = zws
            wide = dot(band, zws, ((1,), (0,)))
            for part in range(2):
                n = 2 * half + part
                at_n = slice(BLOCK * n, BLOCK * (n + 1))
                lanes = slice(LANES * part, LANES * (part + 1))
                m = wide[0:BLOCK, lanes]
                for g in range(1, per_tile):
                    m = jnp.where(picks[g], wide[BLOCK * g : BLOCK * (g + 1), lanes], m)
                um_ref[tile, at_n] = up_ref[at_n, at].astype(F32) * m

    in_groups(tiles, beside, (filters, medium))


def backward_kernel(
    all_channels,
    beside,
    count,
    xk_ref,
    ks_ref,
    xq_ref,
    xk_first_ref,
    xv_ref,
    ks_first_ref,
    vs_ref,
    zw_ref,
    uq_ref,
    um_ref,
    note_ref,
    band_t_ref,
    *rest,
):
    *sq_refs, out_ref, dm_ref, dz_ref, skew_ref, w_ref = rest
    tiles, rows = uq_ref.shape[0:2]
    own = rows // BLOCK
    window = xv_ref.shape[1] // SLOT
    span = window - own
    per_tile = band_t_ref.shape[2] // BLOCK
    _, same, reward = notes_of(note_ref, own, span)
    masks = [jnp.where(pick, 1.0, 0.0).astype(BF16) for pick in lane_picks(per_tile)]
    weight = reward * lax.rsqrt(summed([ref[0:1] for ref in sq_refs]) / all_channels + 1e-06)
    w_ref[...] = jnp.broadcast_to(weight, (LANES, rows)).T

    def fold(x):
        return jnp.sum(x.reshape(BLOCK // 8, 8, LANES), axis=0)

    def stack(tile, side, _):
        for n in range(own):
            at_n = slice(BLOCK * n, BLOCK * (n + 1))
            dm = (w_ref[at_n] * uq_ref[tile, at_n]).astype(BF16)
            lanes = slice(LANES * (n % 2), LANES * (n % 2 + 1))
            for g in range(per_tile):
                dm_ref[side, n // 2, BLOCK * g : BLOCK * (g + 1), lanes] = dm * masks[g]

    def middle(tile, side, _):
        band_t = band_t_ref[tile]
        pair = None
        for half in range(own // 2):
            dms = dm_ref[side, half]
            back = dot(band_t, dms, ((1,), (0,)))
            both = dot(dms, zw_ref[tile, half], ((1,), (1,)))
            pair = both if pair is None else pair + both
            for part in range(2):
                n = 2 * half + part
                lanes = slice(LANES * part, LANES * (part + 1))
                for s in range(span + 1):
                    at_s = slice(BLOCK * (n + s), BLOCK * (n + s + 1))
                    term = back[BLOCK * s : BLOCK * (s + 1), lanes]
                    if s < span:
                        term = term * same[n][s]
                    if n == 0 or s == span:
                        dz_ref[side, at_s] = term
                    else:
                        dz_ref[side, at_s] += term
        lined = pair.reshape(per_tile, BLOCK // 8, 8, 2 * LANES)
        skew = None
        for r in range(BLOCK // 8):
            rows_r = lined[:, r].reshape(per_tile * 8, 2 * LANES)
            moved = pltpu.roll(rows_r, 2 * LANES - 8 * r, 1) if r else rows_r
            skew = moved if skew is None else skew + moved
        for side_of in range(2):
            start = (side_of * tiles + tile) * per_tile * 8
            skew_ref[pl.ds(pl.multiple_of(start, 8), per_tile * 8)] = skew[
                :, LANES * side_of : LANES * (side_of + 1)
            ]

    def grads(tile, side, _):
        at = tile_lanes(tile)
        gq, gk, gv = ([jnp.zeros((8, LANES), F32) for _ in range(count)] for _ in range(3))
        for n in range(own):
            at_n = slice(BLOCK * n, BLOCK * (n + 1))
            cot_q = w_ref[at_n] * um_ref[tile, at_n]
            for j in range(count):
                gq[j] = gq[j] + fold(cot_q * shifted(xq_ref, tile, n, j))
        for b in range(window):
            at_b = slice(BLOCK * b, BLOCK * (b + 1))
            dz = dz_ref[side, at_b]
            cot_k = dz * vs_ref[tile, at_b]
            ks = ks_ref[tile, BLOCK * (b - 1) : BLOCK * b] if b else ks_first_ref[tile]
            cot_v = dz * ks
            for j in range(count):
                k_rows = shifted(xk_ref, tile, b - 1, j) if b else shifted(xk_first_ref, tile, 0, j)
                gk[j] = gk[j] + fold(cot_k * k_rows)
                gv[j] = gv[j] + fold(cot_v * shifted(xv_ref, tile, b, j))
        for i, sums in enumerate((gq, gk, gv)):
            for j in range(count):
                out_ref[8 * i + j : 8 * i + j + 1, at] = jnp.sum(sums[j], axis=0, keepdims=True)
            out_ref[8 * i + count : 8 * i + 8, at] = jnp.zeros((8 - count, LANES), F32)

    in_groups(tiles, beside, (stack, middle, grads))
    lane = lax.broadcasted_iota(jnp.int32, (2 * LANES, LANES), 0)
    tap = lax.broadcasted_iota(jnp.int32, (2 * LANES, LANES), 1)
    groups = tiles * per_tile
    totals = None
    for u in range(8):
        rows_u = jnp.concatenate(
            [skew_ref[pl.ds(8 * groups * i + u, groups, stride=8)] for i in range(2)], axis=1
        )
        high = rows_u.astype(BF16)
        low = (rows_u - high.astype(F32)).astype(BF16)
        pick = jnp.where(lane + tap == LANES + u, 1.0, 0.0).astype(BF16)
        term = dot(jnp.concatenate([high, low], axis=0), pick, ((1,), (0,)))
        totals = term if totals is None else totals + term
    totals = totals[0:groups] + totals[groups:]
    for tile in range(tiles):
        out_ref[24 : 24 + per_tile, LANES * tile : LANES * (tile + 1)] = totals[
            per_tile * tile : per_tile * (tile + 1)
        ]


def last_kernel(scale, *refs):
    *part_refs, se_ref, mr_ref, se_here, mr_here, sems = refs
    tap_count, channels = se_here.shape[1:]

    def total_of(rows):
        return summed([ref[rows].astype(F32) for ref in part_refs]) * scale

    low = total_of(slice(24, None))
    mr_here[...] = jnp.concatenate(
        [low[:, t * LANES : (t + 1) * LANES] for t in range(channels // LANES)], axis=0
    )
    copies = [pltpu.make_async_copy(mr_here, mr_ref, sems.at[3])]
    copies[0].start()
    for i in range(3):
        se_here[i] = total_of(slice(8 * i, 8 * (i + 1)))[0:tap_count]
        copy = pltpu.make_async_copy(se_here.at[i], se_ref.at[i], sems.at[i])
        copy.start()
        copies.append(copy)
    for copy in copies:
        copy.wait()


def swapped(value, axis, distance):
    count = lax.axis_size(axis)
    return lax.ppermute(value, axis, [(i, i ^ distance) for i in range(count)])


def summed_small(value, axis, beside):
    count = lax.axis_size(axis)
    if count & (count - 1):
        return [lax.psum(value, axis)], beside
    distance = 1
    while 2 * distance < count:
        got = swapped(value, axis, distance)
        if distance == 1:
            got, beside = lax.optimization_barrier((got, beside))
        value = value + got
        distance *= 2
    return [value, swapped(value, axis, distance)], beside


def spread(part, axis):
    count = lax.axis_size(axis)
    if count & (count - 1) or count < 8:
        return [lax.psum(part, axis)]
    mine = (part + swapped(part, axis, 1)).astype(BF16)
    distance = 8
    while distance < count:
        mine = (mine.astype(F32) + swapped(mine, axis, distance).astype(F32)).astype(BF16)
        distance *= 2
    return [mine] + [swapped(mine, axis, d) for d in (2, 4, 6)]


def moved_up(value, axis, steps):
    count = lax.axis_size(axis)
    return lax.ppermute(value, axis, [(i, (i + steps) % count) for i in range(count)])


def on_device(query, key, value, upstream, reward, lengths, se_filter, mr_filter):
    rows, channels = query.shape
    taps, groups = mr_filter.shape
    tap_count = se_filter.shape[1]
    tiles = channels // LANES
    per_tile = groups // tiles
    stack = per_tile * BLOCK
    own = rows // BLOCK
    span = taps // BLOCK
    window = own + span
    beside = math.gcd(tiles, 8)
    dp = lax.axis_size("dp")

    k_near = moved_up(key, "dp", 1)
    near, far, sq, notes, medium_taps, short_taps = pl.pallas_call(
        functools.partial(first_kernel, span),
        out_shape=(
            jax.ShapeDtypeStruct((rows + TAIL, channels), BF16),
            jax.ShapeDtypeStruct((2 * PRE, channels), BF16),
            jax.ShapeDtypeStruct((COPIES, rows), F32),
            jax.ShapeDtypeStruct((window + own * span + 1, rows), F32),
            jax.ShapeDtypeStruct((groups, taps), BF16),
            jax.ShapeDtypeStruct(se_filter.shape, BF16),
        ),
        in_specs=[spec(pl.ANY)] * 8,
        out_specs=(spec(),) * 6,
        scratch_shapes=[
            pltpu.VMEM((rows, channels), BF16),
            pltpu.VMEM((TAIL, channels), BF16),
            pltpu.SMEM(lengths.shape, jnp.int32),
            pltpu.VMEM((1, rows), jnp.int32),
            pltpu.SemaphoreType.DMA((8,)),
        ],
        compiler_params=pltpu.CompilerParams(vmem_limit_bytes=LIMIT),
        cost_estimate=cost(1.2),
        name="first",
    )(
        *[
            pltpu.with_memory_space_constraint(x, pltpu.HBM)
            for x in (
                lengths,
                reward.reshape(1, rows),
                query,
                key,
                value,
                upstream,
                mr_filter.T,
                se_filter,
            )
        ]
    )
    near = moved_up(near, "dp", 1)
    far = moved_up(far, "dp", 2)

    band, band_t = pl.pallas_call(
        band_kernel,
        out_shape=(
            jax.ShapeDtypeStruct((tiles, stack, 2 * LANES), BF16),
            jax.ShapeDtypeStruct((tiles, taps + BLOCK, stack), BF16),
        ),
        in_specs=[spec()],
        out_specs=(spec(),) * 2,
        scratch_shapes=[pltpu.VMEM((groups, 2 * LANES), F32)],
        compiler_params=pltpu.CompilerParams(vmem_limit_bytes=LIMIT),
        cost_estimate=cost(1.0),
        name="band",
    )(medium_taps)

    squares, (band, band_t, k_near) = summed_small(sq, "fsdp", (band, band_t, k_near))
    keys = pl.pallas_call(
        functools.partial(key_kernel, beside),
        out_shape=(
            jax.ShapeDtypeStruct((tiles, (window - 1) * SLOT, LANES), F32),
            jax.ShapeDtypeStruct((tiles, (window - 1) * BLOCK, LANES), F32),
        ),
        in_specs=[spec()] * 4,
        out_specs=(spec(),) * 2,
        compiler_params=pltpu.CompilerParams(vmem_limit_bytes=LIMIT),
        cost_estimate=cost(0.5),
        name="keys",
    )(key, k_near, notes, short_taps)
    kept = pl.pallas_call(
        functools.partial(forward_kernel, beside),
        out_shape=(
            jax.ShapeDtypeStruct((tiles, own * SLOT, LANES), F32),
            jax.ShapeDtypeStruct((tiles, SLOT, LANES), F32),
            jax.ShapeDtypeStruct((tiles, window * SLOT, LANES), F32),
            jax.ShapeDtypeStruct((tiles, BLOCK, LANES), F32),
            jax.ShapeDtypeStruct((tiles, window * BLOCK, LANES), F32),
            jax.ShapeDtypeStruct((tiles, own // 2, 2 * LANES, 2 * LANES), BF16),
            jax.ShapeDtypeStruct((tiles, rows, LANES), F32),
            jax.ShapeDtypeStruct((tiles, rows, LANES), F32),
        ),
        in_specs=[spec()] * 10,
        out_specs=(spec(),) * 8,
        scratch_shapes=[pltpu.VMEM((beside, window * BLOCK, LANES), BF16)],
        compiler_params=pltpu.CompilerParams(vmem_limit_bytes=LIMIT),
        cost_estimate=cost(2.0),
        name="forward",
    )(query, value, upstream, k_near, near, far, notes, short_taps, band, keys[1])
    part = pl.pallas_call(
        functools.partial(
            backward_kernel, float(channels * lax.axis_size("fsdp")), beside, tap_count
        ),
        out_shape=jax.ShapeDtypeStruct((24 + per_tile, channels), F32),
        in_specs=[spec()] * (12 + len(squares)),
        out_specs=spec(),
        scratch_shapes=[
            pltpu.VMEM((beside, own // 2, stack, 2 * LANES), BF16),
            pltpu.VMEM((beside, window * BLOCK, LANES), F32),
            pltpu.VMEM((2 * groups * 8 + 8, LANES), F32),
            pltpu.VMEM((rows, LANES), F32),
        ],
        compiler_params=pltpu.CompilerParams(vmem_limit_bytes=LIMIT),
        name="backward",
    )(*keys, *kept, notes, band_t, *squares)

    parts = spread(part, "dp")
    grad_se, grad_mr = pl.pallas_call(
        functools.partial(last_kernel, 1.0 / rows),
        out_shape=(
            jax.ShapeDtypeStruct((3, tap_count, channels), F32),
            jax.ShapeDtypeStruct((groups, taps), F32),
        ),
        in_specs=[spec()] * len(parts),
        out_specs=(spec(pl.ANY),) * 2,
        scratch_shapes=[
            pltpu.VMEM((3, tap_count, channels), F32),
            pltpu.VMEM((groups, taps), F32),
            pltpu.SemaphoreType.DMA((4,)),
        ],
        compiler_params=pltpu.CompilerParams(vmem_limit_bytes=LIMIT),
        name="last",
    )(*parts)
    return grad_se, grad_mr.T


def solution(mesh):
    in_specs = (
        P("dp", "fsdp"),
        P("dp", "fsdp"),
        P("dp", "fsdp"),
        P("dp", "fsdp"),
        P("dp"),
        P(),
        P(None, None, "fsdp"),
        P(None, "fsdp"),
    )
    out_specs = (P(None, None, "fsdp"), P(None, "fsdp"))
    return jax.shard_map(
        on_device, mesh=mesh, in_specs=in_specs, out_specs=out_specs, check_vma=False
    )
```
